128 devices in a mesh: row: 16 (over x, z), col: 8 (over y, core).
Axes of the slice: x: 4, y: 4, z: 4, core: 2. Of those that a mesh axis runs over, the one named last changes fastest.
Arguments:
- momentum: float32 [12288, 16384], P('row', 'col')
- gradient: bfloat16 [12288, 16384], P('row', 'col'), may hold values from -4 to 4
- factor: float32 [16384, 512], P('col'), may hold values from -6 to 6
- serve_perm: int32 [96], replicated, may hold values from 0 to 95, as said below
Outputs:
- new_momentum: float32 [12288, 16384], P('row', 'col')
- new_factor: float32 [16384, 512], P('col')
- served: float32 [12288, 16384], P('row', 'col')
The draws below stay inside these ranges and needn't reach their ends.
Inputs may be any that keep to these rules, and one draw needn't show every extreme that they name: `serve_perm`: A permutation of the 96 blocks. Serving blocks at even positions within a device's 6 blocks come from the first half of the rows (gate), odd ones from the second half (up). The blocks that stand on one index of row go to 6 different indices of row, and each index of row receives from 6 different ones.
All inputs are finite; a program needn't handle non-finite values.
Results may differ from the reference program's by a relative error of at most 0.0003.
Values sent between devices are 32-bit elements; how exact they have to be, the bound alone decides.
A program may use at most 192 MiB of HBM per device.

```python
import math
import jax
import jax.numpy as jnp
from jax import lax

N = 16384
RANK = 512
BLOCK = 128
ROWS = 12288
NBLK = 96
BLK_DEV = 6
N_ROW = 16


def draw_momentum(key, part):
    key = jax.random.fold_in(key, 11)
    key_a, key_b = jax.random.split(key, 2)
    rowfac = jnp.exp(math.log(3.0) * jnp.arange(ROWS, dtype=jnp.float32) / ROWS)
    colfac = jnp.exp(math.log(3.0) * jnp.arange(N, dtype=jnp.float32) / N)
    colfac = colfac * jnp.exp(jax.random.uniform(key_b, (N,), jnp.float32, 0.0, math.log(10.0)))
    base = jax.random.normal(key_a, (ROWS, N), jnp.float32)
    return 0.3 * base * rowfac[:, None] * colfac[None, :]


def draw_serve_perm(key, part):
    key = jax.random.fold_in(key, 12)
    key_a, key_b, key_c = jax.random.split(key, 3)
    half = N_ROW // 2
    pairs = BLK_DEV // 2
    relabel = jax.random.permutation(key_a, N_ROW)
    gate_off = jax.random.permutation(key_b, half)[:pairs]
    up_off = jax.random.permutation(key_c, half)[:pairs]
    dest = jnp.arange(N_ROW, dtype=jnp.int32)[:, None]
    slot = jnp.arange(BLK_DEV, dtype=jnp.int32)[None, :]
    pair = slot // 2
    side = slot % 2
    label = relabel[dest]
    offset = jnp.where(side == 0, gate_off[pair], up_off[pair])
    source = side * half + (label + offset) % half
    local = label // half * pairs + pair
    return (source * BLK_DEV + local).reshape(-1).astype(jnp.int32)


def level_of(rng, extent, cuts, low, top_value):
    loudness, own = 1.0, jax.random.fold_in(rng, 6)
    for dim, blocks in cuts:
        draws = jnp.exp(jax.random.uniform(jax.random.fold_in(own, dim), (blocks,), jnp.float32, low / len(cuts), top_value / len(cuts)))
        loudness = loudness * jnp.repeat(draws, extent[dim] // blocks).reshape([-1 if axis == dim else 1 for axis in range(len(extent))])
    return loudness


def bell_draw(rng, shape, width, limit, cuts=(), held_as=jnp.bfloat16):
    gain = level_of(rng, shape, cuts, -0.22, 0.18) if cuts else 1.0
    entries = jax.random.normal(rng, shape, jnp.float32) * width * gain
    return jnp.minimum(jnp.maximum(entries, -limit), limit).astype(held_as)


def setup_inputs(seed: int = 0) -> dict:
    streams_of = jax.random.split(jax.random.key(seed), 5)
    momentum = draw_momentum(jax.random.fold_in(streams_of[4], 71), 0)
    gradient = bell_draw(streams_of[1], (ROWS, N), 0.3, 4.0, ((0, 16), (1, 8)))
    factor = bell_draw(streams_of[2], (N, RANK), 1.0, 6.0, ((0, 8),), jnp.float32)
    serve_perm = draw_serve_perm(jax.random.fold_in(streams_of[4], 71), 0)
    return dict(momentum=momentum, gradient=gradient, factor=factor, serve_perm=serve_perm)


learn_rate = 0.01

def mult(left, right):
    return jnp.dot(left.astype(jnp.float32), right.astype(jnp.float32), precision=lax.Precision.HIGHEST, preferred_element_type=jnp.float32)

def reference(momentum, gradient, factor, serve_perm):
    buffer = momentum + gradient.astype(jnp.float32)
    power = mult(buffer, factor)
    gram = mult(power.T, power)
    lower = jnp.linalg.cholesky(gram)
    ortho = lax.linalg.triangular_solve(lower, power, left_side=False, lower=True, transpose_a=True)
    right = mult(buffer.T, ortho)
    new_momentum = buffer - 0.05 * mult(ortho, right.T)
    colsq = lax.optimization_barrier(jnp.sum(right * right, axis=0))
    new_factor = right / jnp.sqrt(colsq + 1e-06)
    coefficient = jnp.float32(learn_rate) * jnp.sqrt(jnp.float32(ROWS) / jnp.float32(N))
    update = -coefficient * mult(ortho, new_factor.T)
    served = update.reshape(NBLK, BLOCK, N)[serve_perm].reshape(ROWS, N)
    return (new_momentum, new_factor, served)
```

```python
import jax
import jax.numpy as jnp
from jax import lax
from jax.experimental import pallas as pl
from jax.experimental.pallas import tpu as pltpu
from jax.sharding import PartitionSpec as P

N = 16384
ROWS = 12288
RANK = 512
learn_rate = 0.01

f32 = jnp.float32
bf16 = jnp.bfloat16
HIGHEST = lax.Precision.HIGHEST
MESH = pl.DeviceIdType.MESH
NN = (((1,), (0,)), ((), ()))
NT = (((1,), (1,)), ((), ()))


def mm(a, b, dims=NN):
    return lax.dot_general(a, b, dims, preferred_element_type=f32)


def mm_exact(a, b, dims=NN):
    return lax.dot_general(a, b, dims, precision=HIGHEST, preferred_element_type=f32)


def split(a):
    high = a.astype(bf16)
    return high, (a - high.astype(f32)).astype(bf16)


def eliminate(block):
    lane = lax.broadcasted_iota(jnp.int32, (8, 128), 1)
    sub = lax.broadcasted_iota(jnp.int32, (8, 128), 0)
    done = []
    rest = block
    for first in range(0, 128, 8):
        height = 128 - first
        cols = [jnp.broadcast_to(rest[:, first + j:first + j + 1], (height, 128)) for j in range(8)]
        inside = (lane >= first) & (lane < first + 8)
        tile = jnp.where(inside, 0.0, rest[:8])
        factors, rows = [], []
        for i in range(8):
            scale = lax.rsqrt(jnp.broadcast_to(cols[i][i:i + 1], (8, 128)))
            column = cols[i] * scale[:1]
            factors.append(column)
            for j in range(i + 1, 8):
                cols[j] = cols[j] - column * column[j:j + 1]
            row = jnp.broadcast_to(jnp.where(lane == first + i, 1.0, tile)[i:i + 1], (8, 128)) * scale
            rows.append(row)
            tile = jnp.where(sub > i, tile - column[:8] * row, jnp.where(sub == i, row, tile))
        done.append(tile)
        if height > 8:
            wide = lax.broadcasted_iota(jnp.int32, (height - 8, 128), 1)
            rest = jnp.where((wide >= first) & (wide < first + 8), 0.0, rest[8:])
            for i in range(8):
                rest = rest - factors[i][8:] * rows[i][:1]
    return jnp.concatenate(done, axis=0)


def fused(perm_ref, mom_hbm, grad_hbm, fac_hbm,
          rt_hi, rt_lo, ortho_out, oph_out, opl_out, scale_out,
          mom, grad, fac, buf_hi, buf_lo, fac_hi, fac_lo, part, from_core, to_y, from_y,
          power, pt_hi, pt_lo, gpart, gfrom, gram, work, zt, zfrom1, zsum1, zfrom2, zo,
          psend, pfrom, ppiece, pperm, csq, cfrom,
          lsem, a1s, a1r, a2s, a2r, bs, br, b2s, b2r, g1s, g1r, g2s, g2r, g3s, g3r, g4s, g4r,
          z1s, z1r, z2s, z2r, z3s, z3r, z4s, z4r, p1s, p1r, p2s, p2r, cs, cr):
    me_row = lax.axis_index("row")
    me_col = lax.axis_index("col")
    x, z = me_row // 4, me_row % 4
    y, core = me_col // 2, me_col % 2
    mate = (me_row, y * 2 + 1 - core)
    pending = []

    def send(src, dst, ssem, rsem, dev):
        copy = pltpu.make_async_remote_copy(src_ref=src, dst_ref=dst, send_sem=ssem, recv_sem=rsem,
                                            device_id=dev, device_id_type=MESH)
        copy.start()
        pending.append(copy)

    def arrive(dst, ssem, rsem):
        pltpu.make_async_remote_copy(src_ref=dst, dst_ref=dst, send_sem=ssem, recv_sem=rsem,
                                     device_id=mate, device_id_type=MESH).wait_recv()

    other = pl.multiple_of((1 - core) * 384, 384)
    mine = pl.multiple_of(core * 384, 384)

    loads = [pltpu.make_async_copy(fac_hbm, fac, lsem.at[0])]
    for h, start in enumerate((other, mine)):
        rows = pl.ds(start, 384)
        loads.append(pltpu.make_async_copy(mom_hbm.at[rows], mom.at[rows], lsem.at[1 + 2 * h]))
        loads.append(pltpu.make_async_copy(grad_hbm.at[rows], grad.at[rows], lsem.at[2 + 2 * h]))
    for copy in loads:
        copy.start()

    barrier = pltpu.get_barrier_semaphore()
    for d in range(1, 16):
        pl.semaphore_signal(barrier, inc=1, device_id=((me_row + d) % 16, me_col), device_id_type=MESH)
    for d in range(1, 8):
        pl.semaphore_signal(barrier, inc=1, device_id=(me_row, (me_col + d) % 8), device_id_type=MESH)

    loads[0].wait()

    @pl.loop(0, 32)
    def _(i):
        rows = pl.ds(pl.multiple_of(i * 64, 64), 64)
        high, low = split(fac[rows, :])
        fac_hi[rows, :] = high
        fac_lo[rows, :] = low

    def power_half(h, start):
        loads[1 + 2 * h].wait()
        loads[2 + 2 * h].wait()

        @pl.loop(0, 12)
        def _(i):
            rows = pl.ds(pl.multiple_of(start + i * 32, 32), 32)
            high, low = split(mom[rows, :] + grad[rows, :].astype(f32))
            buf_hi[rows, :] = high
            buf_lo[rows, :] = low

        rows = pl.ds(start, 384)
        part[rows, :] = (mm(buf_hi[rows, :], fac_hi[...]) + mm(buf_hi[rows, :], fac_lo[...])
                         + mm(buf_lo[rows, :], fac_hi[...]))

    power_half(0, other)
    pl.semaphore_wait(barrier, 22)
    for d in (2, 1, 3, 0):
        to = (y + d) % 4
        send(part.at[pl.ds(pl.multiple_of(other + to * 96, 96), 96)], from_core.at[to],
             a1s.at[d], a1r.at[to], mate)
    power_half(1, mine)
    for d in (2, 1, 3):
        to = (y + d) % 4
        arrive(from_core.at[to], a1s.at[d], a1r.at[to])
        to_y[to] = part[pl.ds(pl.multiple_of(mine + to * 96, 96), 96), :] + from_core[to]
        send(to_y.at[to], from_y.at[y], a2s.at[d], a2r.at[y], (me_row, to * 2 + core))
    arrive(from_core.at[y], a1s.at[0], a1r.at[y])
    own = part[pl.ds(pl.multiple_of(mine + y * 96, 96), 96), :] + from_core[y]
    for d in (1, 3, 2):
        src = (y + d) % 4
        arrive(from_y.at[src], a2s.at[d], a2r.at[src])
        own = own + from_y[src]
    here = pl.ds(pl.multiple_of(mine + y * 96, 96), 96)
    power[here, :] = own
    for d in (2, 1, 3):
        to = (y + d) % 4
        send(power.at[here], power.at[here], bs.at[d], br.at[y], (me_row, to * 2 + core))
    send(power.at[here], power.at[here], b2s.at[0], b2r.at[y], mate)
    for d in (1, 3, 2):
        src = (y + d) % 4
        there = pl.ds(pl.multiple_of(mine + src * 96, 96), 96)
        arrive(power.at[there], bs.at[d], br.at[src])
        send(power.at[there], power.at[there], b2s.at[d], b2r.at[src], mate)
    for d in (0, 1, 3, 2):
        src = (y + d) % 4
        there = pl.ds(pl.multiple_of(other + src * 96, 96), 96)
        arrive(power.at[there], b2s.at[d], b2r.at[src])

    for j in range(6):
        high, low = split(power[j * 128:j * 128 + 128, :].T)
        pt_hi[:, j * 128:j * 128 + 128] = high
        pt_lo[:, j * 128:j * 128 + 128] = low

    strip = pl.ds(pl.multiple_of(me_col * 64, 64), 64)
    p_hi, p_lo = pt_hi[strip, :], pt_lo[strip, :]
    gpart[...] = (mm(p_hi, pt_hi[...], NT) + mm(p_hi, pt_lo[...], NT)
                  + mm(p_lo, pt_hi[...], NT) + mm(p_lo, pt_lo[...], NT))

    def unit(r, base=0):
        return (pl.ds(pl.multiple_of(base + (r // 2) * 8, 8), 8), pl.ds(pl.multiple_of((r % 2) * 256, 256), 256))

    for d in range(1, 16):
        to = (me_row + d) % 16
        send(gpart.at[unit(to)], gfrom.at[me_row], g1s.at[d], g1r.at[me_row], (to, me_col))

    def pick(dest):
        local = jnp.int32(0)
        for t in range(6):
            b = perm_ref[dest * 6 + t] - me_row * 6
            local = local + jnp.where((b >= 0) & (b < 6), b, 0)
        share = power[pl.ds(pl.multiple_of(me_col * 16, 16), 16), :]
        for l in range(1, 6):
            share = jnp.where(local == l, power[pl.ds(pl.multiple_of(l * 128 + me_col * 16, 16), 16), :], share)
        return share

    for d in range(1, 16):
        to = (me_row + d) % 16
        psend[d] = pick(to)
    pfrom[me_row] = pick(me_row)

    def z_half(h):
        @pl.loop(0, 2)
        def _(t):
            cols = pl.ds(pl.multiple_of(h * 1024 + t * 512, 512), 512)
            zt[h, :, pl.ds(pl.multiple_of(t * 512, 512), 512)] = (
                mm(pt_hi[...], buf_hi[:, cols]) + mm(pt_hi[...], buf_lo[:, cols])
                + mm(pt_lo[...], buf_hi[:, cols]))

    z_half(0)
    total = gpart[unit(me_row)]
    for d in range(1, 16):
        src = (me_row + d) % 16
        arrive(gfrom.at[src], g1s.at[d], g1r.at[src])
        total = total + gfrom[src]
    gram[unit(me_row, me_col * 64)] = total
    for d in range(1, 16):
        to = (me_row + d) % 16
        piece = gram.at[unit(me_row, me_col * 64)]
        send(piece, piece, g2s.at[d], g2r.at[me_row], (to, me_col))
    z_half(1)
    for d in range(1, 16):
        src = (me_row + d) % 16
        arrive(gram.at[unit(src, me_col * 64)], g2s.at[d], g2r.at[src])

    def strip_of(c):
        return pl.ds(pl.multiple_of(c * 64, 64), 64)

    for d in (2, 1, 3):
        to = (y + d) % 4
        send(gram.at[strip], gram.at[strip], g3s.at[d], g3r.at[y], (me_row, to * 2 + core))
    send(gram.at[strip], gram.at[strip], g4s.at[0], g4r.at[y], mate)

    axes = ((x, z), (z, x))

    def peer(h, level, to):
        along_x = (h == 0) == (level == 0)
        return (to * 4 + z, me_col) if along_x else (x * 4 + to, me_col)

    for d in (2, 1, 3):
        for h in range(2):
            a, b = axes[h]
            to = (a + d) % 4
            send(zt.at[h, pl.ds(pl.multiple_of(to * 128, 128), 128)], zfrom1.at[h, a],
                 z1s.at[h, d], z1r.at[h, a], peer(h, 0, to))
    for d in range(1, 16):
        to = (me_row + d) % 16
        send(psend.at[d], pfrom.at[me_row], p1s.at[d], p1r.at[me_row], (to, me_col))

    for d in (1, 3, 2):
        src = (y + d) % 4
        there = strip_of(src * 2 + core)
        arrive(gram.at[there], g3s.at[d], g3r.at[src])
        send(gram.at[there], gram.at[there], g4s.at[d], g4r.at[src], mate)
    for d in (0, 1, 3, 2):
        src = (y + d) % 4
        arrive(gram.at[strip_of(src * 2 + 1 - core)], g4s.at[d], g4r.at[src])

    def z_second():
        for h in range(2):
            a, b = axes[h]
            total = zt[h, pl.ds(pl.multiple_of(a * 128, 128), 128), :]
            for d in (1, 3, 2):
                src = (a + d) % 4
                arrive(zfrom1.at[h, src], z1s.at[h, d], z1r.at[h, src])
                total = total + zfrom1[h, src]
            zsum1[h] = total
            for d in (2, 1, 3):
                to = (b + d) % 4
                send(zsum1.at[h, pl.ds(pl.multiple_of(to * 32, 32), 32)], zfrom2.at[h, b],
                     z2s.at[h, d], z2r.at[h, b], peer(h, 1, to))

    def place(h, b):
        return pl.ds(pl.multiple_of(axes[h][0] * 128 + b * 32, 32), 32)

    def z_third():
        for h in range(2):
            a, b = axes[h]
            total = zsum1[h, pl.ds(pl.multiple_of(b * 32, 32), 32), :]
            for d in (1, 3, 2):
                src = (b + d) % 4
                arrive(zfrom2.at[h, src], z2s.at[h, d], z2r.at[h, src])
                total = total + zfrom2[h, src]
            zo[h, place(h, b), :] = total
            for d in (2, 1, 3):
                to = (b + d) % 4
                piece = zo.at[h, place(h, b)]
                send(piece, piece, z3s.at[h, d], z3r.at[h, b], peer(h, 1, to))

    def z_fourth():
        for h in range(2):
            a, b = axes[h]
            for d in (1, 3, 2):
                src = (b + d) % 4
                arrive(zo.at[h, place(h, src)], z3s.at[h, d], z3r.at[h, src])
            piece = zo.at[h, pl.ds(pl.multiple_of(a * 128, 128), 128)]
            for d in (2, 1, 3):
                to = (a + d) % 4
                send(piece, piece, z4s.at[h, d], z4r.at[h, a], peer(h, 0, to))

    def perm_second():
        for t in range(6):
            first = perm_ref[me_row * 6 + t]
            share = pfrom[0]
            for r in range(1, 16):
                share = jnp.where(first >= r * 6, pfrom[r], share)
            ppiece[t] = share
        mine_rows = pl.ds(pl.multiple_of(me_col * 16, 16), 16)
        pperm[:, mine_rows, :] = ppiece[...]
        for d in range(1, 8):
            to = (me_col + d) % 8
            send(ppiece, pperm.at[:, mine_rows], p2s.at[d], p2r.at[me_col], (me_row, to))

    li = lax.broadcasted_iota(jnp.int32, (128, 128), 0)
    lj = lax.broadcasted_iota(jnp.int32, (128, 128), 1)

    work[...] = gram[...]
    for k in range(4):
        s = slice(128 * k, 128 * k + 128)
        inv = jnp.where(li >= lj, eliminate(work[s, s]), 0.0)
        work[s, s] = jnp.where(li == lj, 1.0, 0.0)
        row = mm_exact(inv, work[s, :])
        work[s, :] = row
        if k < 3:
            r = slice(128 * k + 128, 512)
            low = mm_exact(work[r, s], inv, NT)
            work[r, s] = jnp.zeros((512 - 128 * k - 128, 128), f32)
            work[r, :] = work[r, :] - mm_exact(low, row)
        if k == 0:
            for d in range(1, 16):
                src = (me_row + d) % 16
                arrive(pfrom.at[src], p1s.at[d], p1r.at[src])
            perm_second()
        if k == 1:
            z_second()
        if k == 2:
            z_third()
        if k == 3:
            z_fourth()

    ii = lax.broadcasted_iota(jnp.int32, (512, 512), 0)
    jj = lax.broadcasted_iota(jnp.int32, (512, 512), 1)
    inv_hi, inv_lo = split(jnp.where(ii >= jj, work[...], 0.0))

    def times_inverse(block):
        high, low = split(block)
        return mm(high, inv_hi, NT) + mm(high, inv_lo, NT) + mm(low, inv_hi, NT)

    ortho_out[...] = (0.05 * times_inverse(power[...])).astype(bf16)
    for d in range(1, 8):
        src = (me_col + d) % 8
        arrive(pperm.at[:, pl.ds(pl.multiple_of(src * 16, 16), 16)], p2s.at[d], p2r.at[src])
    served = times_inverse(pperm[...].reshape(768, 512))

    for h in range(2):
        a, b = axes[h]
        for d in (1, 3, 2):
            src = (a + d) % 4
            arrive(zo.at[h, pl.ds(pl.multiple_of(src * 128, 128), 128)], z4s.at[h, d], z4r.at[h, src])

    squares = jnp.zeros((512, 1), f32)
    for h in range(2):
        for t in range(2):
            z_hi, z_lo = split(zo[h, :, t * 512:t * 512 + 512])
            right = mm(inv_hi, z_hi) + mm(inv_hi, z_lo) + mm(inv_lo, z_hi)
            high, low = split(right)
            cols = slice(h * 1024 + t * 512, h * 1024 + t * 512 + 512)
            rt_hi[:, cols] = high
            rt_lo[:, cols] = low
            squares = squares + jnp.sum(right * right, axis=1, keepdims=True)
    flat = jnp.sum(jnp.where(ii == jj, squares, 0.0), axis=0, keepdims=True)
    csq[...] = jnp.broadcast_to(flat, (8, 512))
    for d in range(1, 8):
        to = (me_col + d) % 8
        send(csq, cfrom.at[me_col], cs.at[d], cr.at[me_col], (me_row, to))
    total = csq[...]
    for d in range(1, 8):
        src = (me_col + d) % 8
        arrive(cfrom.at[src], cs.at[d], cr.at[src])
        total = total + cfrom[src]
    scale = 1.0 / jnp.sqrt(total + 1e-06)
    scale_out[...] = scale
    coefficient = learn_rate * (ROWS / N) ** 0.5
    high, low = split(served * (-coefficient * scale[:1]))
    oph_out[...] = high
    opl_out[...] = low

    for copy in pending:
        copy.wait_send()


def finish(mom, grad, ortho, oph, opl, rt_hi, rt_lo, scale, new_mom, new_fac, served):
    r_hi, r_lo = rt_hi[...], rt_lo[...]
    new_mom[...] = mom[...] + grad[...].astype(f32) - mm(ortho[...], r_hi)
    served[...] = mm(oph[...], r_hi) + mm(oph[...], r_lo) + mm(opl[...], r_hi)
    new_fac[...] = (r_hi.astype(f32) + r_lo.astype(f32)).T * scale[:1]


def body(momentum, gradient, factor, serve_perm):
    vmem = pl.BlockSpec(memory_space=pltpu.VMEM)
    anywhere = pl.BlockSpec(memory_space=pl.ANY)
    V = pltpu.VMEM
    D = pltpu.SemaphoreType.DMA
    shape = jax.ShapeDtypeStruct
    rt_hi, rt_lo, ortho, oph, opl, scale = pl.pallas_call(
        fused,
        out_shape=(shape((512, 2048), bf16), shape((512, 2048), bf16), shape((768, 512), bf16),
                   shape((768, 512), bf16), shape((768, 512), bf16), shape((8, 512), f32)),
        in_specs=[pl.BlockSpec(memory_space=pltpu.SMEM), anywhere, anywhere, anywhere],
        out_specs=(vmem,) * 6,
        scratch_shapes=[
            V((768, 2048), f32), V((768, 2048), bf16), V((2048, 512), f32),
            V((768, 2048), bf16), V((768, 2048), bf16), V((2048, 512), bf16), V((2048, 512), bf16),
            V((768, 512), f32), V((4, 96, 512), f32), V((4, 96, 512), f32), V((4, 96, 512), f32),
            V((768, 512), f32), V((512, 768), bf16), V((512, 768), bf16),
            V((64, 512), f32), V((16, 8, 256), f32), V((512, 512), f32), V((512, 512), f32),
            V((2, 512, 1024), f32), V((2, 4, 128, 1024), f32), V((2, 128, 1024), f32),
            V((2, 4, 32, 1024), f32), V((2, 512, 1024), f32),
            V((16, 16, 512), f32), V((16, 16, 512), f32), V((6, 16, 512), f32), V((6, 128, 512), f32),
            V((8, 512), f32), V((8, 8, 512), f32),
            D((5,)), D((4,)), D((4,)), D((4,)), D((4,)), D((4,)), D((4,)), D((4,)), D((4,)),
            D((16,)), D((16,)), D((16,)), D((16,)), D((4,)), D((4,)), D((4,)), D((4,)),
            D((2, 4)), D((2, 4)), D((2, 4)), D((2, 4)), D((2, 4)), D((2, 4)), D((2, 4)), D((2, 4)),
            D((16,)), D((16,)), D((8,)), D((8,)), D((8,)), D((8,)),
        ],
        compiler_params=pltpu.CompilerParams(
            collective_id=0, has_side_effects=True, vmem_limit_bytes=60 * 1024 * 1024),
        name="factorize",
    )(serve_perm, momentum, gradient, factor)

    def tall(i):
        return (0, i)

    def whole(i):
        return (0, 0)

    return pl.pallas_call(
        finish,
        grid=(8,),
        out_shape=(shape((768, 2048), f32), shape((2048, 512), f32), shape((768, 2048), f32)),
        in_specs=[pl.BlockSpec((768, 256), tall), pl.BlockSpec((768, 256), tall),
                  pl.BlockSpec((768, 512), whole), pl.BlockSpec((768, 512), whole),
                  pl.BlockSpec((768, 512), whole),
                  pl.BlockSpec((512, 256), tall), pl.BlockSpec((512, 256), tall),
                  pl.BlockSpec((8, 512), whole)],
        out_specs=(pl.BlockSpec((768, 256), tall), pl.BlockSpec((256, 512), lambda i: (i, 0)),
                   pl.BlockSpec((768, 256), tall)),
        compiler_params=pltpu.CompilerParams(vmem_limit_bytes=60 * 1024 * 1024),
        cost_estimate=pl.CostEstimate(flops=8 * 768 * 2048 * 512, bytes_accessed=30 * 2**20, transcendentals=0),
        name="outputs",
    )(momentum, gradient, ortho, oph, opl, rt_hi, rt_lo, scale)


def solution(mesh):
    return jax.shard_map(
        body,
        mesh=mesh,
        in_specs=(P("row", "col"), P("row", "col"), P("col", None), P()),
        out_specs=(P("row", "col"), P("col", None), P("row", "col")),
        check_vma=False,
    )
```

```python
import jax
import jax.numpy as jnp
from jax import lax
from jax.experimental import pallas as pl
from jax.experimental.pallas import tpu as pltpu
from jax.sharding import PartitionSpec as P

N = 16384
ROWS = 12288
RANK = 512
learn_rate = 0.01

f32 = jnp.float32
bf16 = jnp.bfloat16
HIGHEST = lax.Precision.HIGHEST
MESH = pl.DeviceIdType.MESH
NN = (((1,), (0,)), ((), ()))
NT = (((1,), (1,)), ((), ()))


def mm(a, b, dims=NN):
    return lax.dot_general(a, b, dims, preferred_element_type=f32)


def mm_exact(a, b, dims=NN):
    return lax.dot_general(a, b, dims, precision=HIGHEST, preferred_element_type=f32)


def split(a):
    high = a.astype(bf16)
    return high, (a - high.astype(f32)).astype(bf16)


def eliminate(block):
    lane = lax.broadcasted_iota(jnp.int32, (8, 128), 1)
    sub = lax.broadcasted_iota(jnp.int32, (8, 128), 0)
    done = []
    rest = block
    for first in range(0, 128, 8):
        height = 128 - first
        cols = [jnp.broadcast_to(rest[:, first + j:first + j + 1], (height, 128)) for j in range(8)]
        inside = (lane >= first) & (lane < first + 8)
        tile = jnp.where(inside, 0.0, rest[:8])
        factors, rows = [], []
        for i in range(8):
            scale = lax.rsqrt(jnp.broadcast_to(cols[i][i:i + 1], (8, 128)))
            column = cols[i] * scale[:1]
            factors.append(column)
            for j in range(i + 1, 8):
                cols[j] = cols[j] - column * column[j:j + 1]
            row = jnp.broadcast_to(jnp.where(lane == first + i, 1.0, tile)[i:i + 1], (8, 128)) * scale
            rows.append(row)
            tile = jnp.where(sub > i, tile - column[:8] * row, jnp.where(sub == i, row, tile))
        done.append(tile)
        if height > 8:
            wide = lax.broadcasted_iota(jnp.int32, (height - 8, 128), 1)
            rest = jnp.where((wide >= first) & (wide < first + 8), 0.0, rest[8:])
            for i in range(8):
                rest = rest - factors[i][8:] * rows[i][:1]
    return jnp.concatenate(done, axis=0)


class Ring:
    def __init__(self, a, peer, ssem, rsem, pending):
        self.a, self.peer, self.ssem, self.rsem, self.pending = a, peer, ssem, rsem, pending
        self.up, self.down, self.far = (a + 1) % 4, (a + 3) % 4, (a + 2) % 4

    def send(self, i, src, dst, to):
        copy = pltpu.make_async_remote_copy(src_ref=src, dst_ref=dst, send_sem=self.ssem(i), recv_sem=self.rsem(i),
                                            device_id=self.peer(to), device_id_type=MESH)
        copy.start()
        self.pending.append(copy)

    def arrive(self, i, dst):
        pltpu.make_async_remote_copy(src_ref=dst, dst_ref=dst, send_sem=self.ssem(i), recv_sem=self.rsem(i),
                                     device_id=self.peer(self.up), device_id_type=MESH).wait_recv()


class Reduce(Ring):
    def bind(self, chunk, relay, land):
        self.chunk, self.relay_ref, self.land = chunk, relay, land
        return self

    def start_far(self):
        self.send(0, self.chunk(self.far, 0), self.relay_ref(0), self.up)
        self.send(1, self.chunk(self.far, 1), self.relay_ref(1), self.down)

    def start_near(self):
        self.send(2, self.chunk(self.up, 1), self.land(0, 1), self.up)
        self.send(3, self.chunk(self.down, 0), self.land(1, 0), self.down)

    def start(self):
        self.start_far()
        self.start_near()

    def relay(self):
        for w, to in ((0, self.up), (1, self.down)):
            ref = self.relay_ref(w)
            self.arrive(w, ref)
            ref[...] = ref[...] + self.chunk(to, w)[...]
            self.send(4 + w, ref, self.land(w, w), to)

    def finish(self, h):
        self.arrive(2 + 1 - h, self.land(1 - h, h))
        self.arrive(4 + h, self.land(h, h))
        return self.chunk(self.a, h)[...] + self.land(0, h)[...] + self.land(1, h)[...]


class Gather(Ring):
    def bind(self, chunk):
        self.chunk = chunk
        return self

    def post(self, i, c, h, to):
        self.send(i, self.chunk(c, h), self.chunk(c, h), to)

    def start(self):
        self.post(0, self.a, 0, self.up)
        self.post(1, self.a, 1, self.down)
        self.post(2, self.a, 1, self.up)
        self.post(3, self.a, 0, self.down)

    def relay(self):
        self.arrive(0, self.chunk(self.down, 0))
        self.post(4, self.down, 0, self.up)
        self.arrive(1, self.chunk(self.up, 1))
        self.post(5, self.up, 1, self.down)

    def finish(self):
        self.arrive(2, self.chunk(self.down, 1))
        self.arrive(3, self.chunk(self.up, 0))
        self.arrive(4, self.chunk(self.far, 0))
        self.arrive(5, self.chunk(self.far, 1))


class DirectReduce(Ring):
    def bind(self, chunk, land):
        self.chunk, self.land = chunk, land
        return self

    def start(self):
        for i, to in enumerate((self.far, self.up, self.down)):
            self.send(i, self.chunk(to), self.land(i), to)

    def finish(self):
        total = self.chunk(self.a)[...]
        for i in (1, 2, 0):
            self.arrive(i, self.land(i))
            total = total + self.land(i)[...]
        return total


class DirectGather(Ring):
    def bind(self, chunk):
        self.chunk = chunk
        return self

    def start(self):
        for i, to in enumerate((self.far, self.up, self.down)):
            self.send(i, self.chunk(self.a), self.chunk(self.a), to)

    def finish(self):
        for i, src in ((1, self.down), (2, self.up), (0, self.far)):
            self.arrive(i, self.chunk(src))


def fused(perm_ref, mom_hbm, grad_hbm, fac_hbm,
          rt_hi_out, rt_lo_out, ortho_out, oph_out, opl_out, scale_out,
          mom, grad, fac, buf_hi, buf_lo, fac_hi, fac_lo, part, from_core, to_y, rel_y, land_y,
          power, pt_hi, pt_lo, gpart, gfrom, gram, work, zt, rel1, land1, zsum1, land2, zo,
          psend, pfrom, ppiece, pperm, csq, cfrom, rt_hi, rt_lo, ortho, oph, opl, scale,
          lsem, a1s, a1r, ys, yr, ms, mr, g1s, g1r, g2s, g2r, g3s, g3r, g4s, g4r,
          zs, zr, p1s, p1r, p2s, p2r, cs, cr, osem):
    me_row = lax.axis_index("row")
    me_col = lax.axis_index("col")
    x, z = me_row // 4, me_row % 4
    y, core = me_col // 2, me_col % 2
    mate = (me_row, y * 2 + 1 - core)
    pending = []

    def send(src, dst, ssem, rsem, dev):
        copy = pltpu.make_async_remote_copy(src_ref=src, dst_ref=dst, send_sem=ssem, recv_sem=rsem,
                                            device_id=dev, device_id_type=MESH)
        copy.start()
        pending.append(copy)

    def arrive(dst, ssem, rsem):
        pltpu.make_async_remote_copy(src_ref=dst, dst_ref=dst, send_sem=ssem, recv_sem=rsem,
                                     device_id=mate, device_id_type=MESH).wait_recv()

    def ds(start, size):
        return pl.ds(pl.multiple_of(start, size), size)

    other = pl.multiple_of((1 - core) * 384, 384)
    mine = pl.multiple_of(core * 384, 384)

    def load(h, k):
        rows = pl.ds(other if h == 0 else mine, 384)
        cols = ds(k * 256, 256)
        copies = [pltpu.make_async_copy(mom_hbm.at[rows, cols], mom.at[rows, cols], lsem.at[h, 0, k]),
                  pltpu.make_async_copy(grad_hbm.at[rows, cols], grad.at[rows, cols], lsem.at[h, 1, k])]
        if h == 0:
            copies.append(pltpu.make_async_copy(fac_hbm.at[cols], fac.at[cols], lsem.at[h, 2, k]))
        return copies

    for h in range(2):
        for k in range(8):
            for copy in load(h, k):
                copy.start()

    barrier = pltpu.get_barrier_semaphore()
    for d in range(1, 16):
        pl.semaphore_signal(barrier, inc=1, device_id=((me_row + d) % 16, me_col), device_id_type=MESH)
    for d in range(1, 8):
        pl.semaphore_signal(barrier, inc=1, device_id=(me_row, (me_col + d) % 8), device_id_type=MESH)

    def cols_of(n):
        return slice(n * 256, n * 256 + 256)

    def prepare(h, k):
        for copy in load(h, k):
            copy.wait()
        rows = pl.ds(other if h == 0 else mine, 384)
        cols = ds(k * 256, 256)
        high, low = split(mom[rows, cols] + grad[rows, cols].astype(f32))
        buf_hi[rows, cols] = high
        buf_lo[rows, cols] = low
        if h == 0:
            high, low = split(fac[cols, :])
            fac_hi[cols, :] = high
            fac_lo[cols, :] = low

    def power_block(h, n, k):
        rows = pl.ds(other if h == 0 else mine, 384)
        cols = ds(k * 256, 256)
        c = cols_of(n)
        part[rows, c] = part[rows, c] + (mm(buf_hi[rows, cols], fac_hi[cols, c])
                                         + mm(buf_hi[rows, cols], fac_lo[cols, c])
                                         + mm(buf_lo[rows, cols], fac_hi[cols, c]))

    def power_part(h, n):
        part[pl.ds(other if h == 0 else mine, 384), cols_of(n)] = jnp.zeros((384, 256), f32)
        if n == 0:
            prepare(h, 0)

        @pl.loop(0, 7)
        def _(k):
            if n == 0:
                prepare(h, k + 1)
            power_block(h, n, k)

        power_block(h, n, 7)

    order = (2, 1, 3, 0)

    def core_start(n):
        for d in order:
            to = (y + d) % 4
            send(part.at[ds(other + to * 96, 96), cols_of(n)], from_core.at[n, to],
                 a1s.at[n, d], a1r.at[n, d], mate)

    def core_add(n, d):
        to = (y + d) % 4
        arrive(from_core.at[n, to], a1s.at[n, d], a1r.at[n, d])
        to_y[n, to] = part[ds(mine + to * 96, 96), cols_of(n)] + from_core[n, to]

    def y_peer(to):
        return (me_row, to * 2 + core)

    def half(c, h, size):
        return ds(c * size * 2 + h * size, size)

    def spot(base, c, h):
        return pl.ds(pl.multiple_of(base + c * 96 + h * 48, 48), 48)

    y_sum = [Reduce(y, y_peer, lambda i, n=n: ys.at[0, n, i], lambda i, n=n: yr.at[0, n, i], pending).bind(
        lambda c, h, n=n: to_y.at[n, c, pl.ds(h * 48, 48)],
        lambda w, n=n: rel_y.at[n, w],
        lambda w, h, n=n: land_y.at[n, w, pl.ds(h * 48, 48)]) for n in range(2)]
    y_all = [Gather(y, y_peer, lambda i, n=n: ys.at[1, n, i], lambda i, n=n: yr.at[1, n, i], pending).bind(
        lambda c, h, n=n: power.at[spot(mine, c, h), cols_of(n)]) for n in range(2)]

    def y_start(n):
        core_add(n, 2)
        y_sum[n].start_far()
        core_add(n, 1)
        core_add(n, 3)
        y_sum[n].start_near()

    def to_mate(n, d, h):
        piece = power.at[spot(mine, (y + d) % 4, h), cols_of(n)]
        send(piece, piece, ms.at[n, d, h], mr.at[n, d, h], mate)

    def y_second(n):
        core_add(n, 0)
        for h in range(2):
            power[spot(mine, y, h), cols_of(n)] = y_sum[n].finish(h)
        y_all[n].start()
        for h in range(2):
            to_mate(n, 0, h)

    def y_third(n):
        y_all[n].relay()
        to_mate(n, 3, 0)
        to_mate(n, 1, 1)

    def y_end(n):
        y_all[n].finish()
        for d, h in ((3, 1), (1, 0), (2, 0), (2, 1)):
            to_mate(n, d, h)
        for d, h in ((0, 0), (0, 1), (3, 0), (1, 1), (3, 1), (1, 0), (2, 0), (2, 1)):
            piece = power.at[spot(other, (y + d) % 4, h), cols_of(n)]
            arrive(piece, ms.at[n, d, h], mr.at[n, d, h])
        for j in range(6):
            high, low = split(power[j * 128:j * 128 + 128, cols_of(n)].T)
            pt_hi[cols_of(n), j * 128:j * 128 + 128] = high
            pt_lo[cols_of(n), j * 128:j * 128 + 128] = low

    axes = ((x, z), (z, x))

    def z_peer(h, level):
        along_x = (h == 0) == (level == 0)
        return lambda to: (to * 4 + z, me_col) if along_x else (x * 4 + to, me_col)

    def z_sems(stage, n, h):
        return (lambda i: zs.at[stage, n, h, i]), (lambda i: zr.at[stage, n, h, i])

    pairs = [(n, h) for n in range(2) for h in range(2)]
    z_one, z_two, z_three, z_four = {}, {}, {}, {}
    for n, h in pairs:
        a, b = axes[h]
        z_one[n, h] = Reduce(a, z_peer(h, 0), *z_sems(0, n, h), pending).bind(
            lambda c, t, n=n, h=h: zt.at[n, h, half(c, t, 32)],
            lambda w, n=n, h=h: rel1.at[n, h, w],
            lambda w, t, n=n, h=h: land1.at[n, h, w, pl.ds(t * 32, 32)])
        z_two[n, h] = DirectReduce(b, z_peer(h, 1), *z_sems(1, n, h), pending).bind(
            lambda c, n=n, h=h: zsum1.at[n, h, ds(c * 16, 16)],
            lambda i, n=n, h=h: land2.at[n, h, i])
        z_three[n, h] = DirectGather(b, z_peer(h, 1), *z_sems(2, n, h), pending).bind(
            lambda c, n=n, h=h, a=a: zo.at[n, h, ds(a * 64 + c * 16, 16)])
        z_four[n, h] = Gather(a, z_peer(h, 0), *z_sems(3, n, h), pending).bind(
            lambda c, t, n=n, h=h: zo.at[n, h, half(c, t, 32)])

    def z_compute(n, h):
        @pl.loop(0, 2)
        def _(t):
            cols = ds(h * 1024 + t * 512, 512)
            zt[n, h, :, ds(t * 512, 512)] = (
                mm(pt_hi[cols_of(n), :], buf_hi[:, cols]) + mm(pt_hi[cols_of(n), :], buf_lo[:, cols])
                + mm(pt_lo[cols_of(n), :], buf_hi[:, cols]))

    def both(table, n):
        for h in range(2):
            table[n, h].relay()

    def starts(table, n):
        for h in range(2):
            table[n, h].start()

    def z_second(n):
        for h in range(2):
            for t in range(2):
                zsum1[n, h, t * 32:t * 32 + 32, :] = z_one[n, h].finish(t)

    def z_third(n):
        for h in range(2):
            a, b = axes[h]
            zo[n, h, ds(a * 64 + b * 16, 16), :] = z_two[n, h].finish()
            z_three[n, h].start()

    def z_fourth(n):
        for h in range(2):
            z_three[n, h].finish()
            z_four[n, h].start()

    def z_end(n):
        for h in range(2):
            z_four[n, h].finish()

    strip = ds(me_col * 64, 64)

    def unit(r, base=0):
        return (ds(base + (r // 2) * 8, 8), ds((r % 2) * 256, 256))

    def gram_start():
        p_hi, p_lo = pt_hi[strip, :], pt_lo[strip, :]
        gpart[...] = (mm(p_hi, pt_hi[...], NT) + mm(p_hi, pt_lo[...], NT)
                      + mm(p_lo, pt_hi[...], NT) + mm(p_lo, pt_lo[...], NT))
        for d in range(1, 16):
            to = (me_row + d) % 16
            send(gpart.at[unit(to)], gfrom.at[me_row], g1s.at[d], g1r.at[me_row], (to, me_col))

    def gram_second():
        total = gpart[unit(me_row)]
        for d in range(1, 16):
            src = (me_row + d) % 16
            arrive(gfrom.at[src], g1s.at[d], g1r.at[src])
            total = total + gfrom[src]
        gram[unit(me_row, me_col * 64)] = total
        for d in range(1, 16):
            to = (me_row + d) % 16
            piece = gram.at[unit(me_row, me_col * 64)]
            send(piece, piece, g2s.at[d], g2r.at[me_row], (to, me_col))

    def strip_half(c, h, k):
        return gram.at[ds((c * 2 + k) * 64 + h * 32, 32)]

    strips = Gather(y, y_peer, lambda i: g3s.at[i], lambda i: g3r.at[i], pending).bind(
        lambda c, h: strip_half(c, h, core))

    def strip_to_mate(d, h):
        piece = strip_half((y + d) % 4, h, core)
        send(piece, piece, g4s.at[d, h], g4r.at[d, h], mate)

    def gram_third():
        for d in range(1, 16):
            src = (me_row + d) % 16
            arrive(gram.at[unit(src, me_col * 64)], g2s.at[d], g2r.at[src])
        strips.start()
        strip_to_mate(0, 0)
        strip_to_mate(0, 1)

    def gram_fourth():
        strips.relay()
        strip_to_mate(3, 0)
        strip_to_mate(1, 1)

    def gram_end():
        strips.finish()
        for d, h in ((3, 1), (1, 0), (2, 0), (2, 1)):
            strip_to_mate(d, h)
        for d, h in ((0, 0), (0, 1), (3, 0), (1, 1), (3, 1), (1, 0), (2, 0), (2, 1)):
            arrive(strip_half((y + d) % 4, h, 1 - core), g4s.at[d, h], g4r.at[d, h])
        work[...] = gram[...]

    def pick(dest):
        local = jnp.int32(0)
        for t in range(6):
            b = perm_ref[dest * 6 + t] - me_row * 6
            local = local + jnp.where((b >= 0) & (b < 6), b, 0)
        share = power[ds(me_col * 16, 16), :]
        for l in range(1, 6):
            share = jnp.where(local == l, power[ds(l * 128 + me_col * 16, 16), :], share)
        return share

    def perm_start():
        for d in range(1, 16):
            to = (me_row + d) % 16
            psend[d] = pick(to)
            send(psend.at[d], pfrom.at[me_row], p1s.at[d], p1r.at[me_row], (to, me_col))
        pfrom[me_row] = pick(me_row)

    def perm_second():
        for d in range(1, 16):
            src = (me_row + d) % 16
            arrive(pfrom.at[src], p1s.at[d], p1r.at[src])
        for t in range(6):
            first = perm_ref[me_row * 6 + t]
            share = pfrom[0]
            for r in range(1, 16):
                share = jnp.where(first >= r * 6, pfrom[r], share)
            ppiece[t] = share
        mine_rows = ds(me_col * 16, 16)
        pperm[:, mine_rows, :] = ppiece[...]
        for d in range(1, 8):
            to = (me_col + d) % 8
            send(ppiece, pperm.at[:, mine_rows], p2s.at[d], p2r.at[me_col], (me_row, to))

    li = lax.broadcasted_iota(jnp.int32, (128, 128), 0)
    lj = lax.broadcasted_iota(jnp.int32, (128, 128), 1)

    def factor_block(k):
        s = slice(128 * k, 128 * k + 128)
        inv = jnp.where(li >= lj, eliminate(work[s, s]), 0.0)
        work[s, s] = jnp.where(li == lj, 1.0, 0.0)
        row = mm_exact(inv, work[s, :])
        work[s, :] = row
        if k < 3:
            r = slice(128 * k + 128, 512)
            low = mm_exact(work[r, s], inv, NT)
            work[r, s] = jnp.zeros((512 - 128 * k - 128, 128), f32)
            work[r, :] = work[r, :] - mm_exact(low, row)

    power_part(0, 0)
    pl.semaphore_wait(barrier, 22)
    core_start(0)
    power_part(1, 0)
    power_part(0, 1)
    core_start(1)
    y_start(0)
    power_part(1, 1)
    y_sum[0].relay()
    y_start(1)
    y_second(0)
    y_sum[1].relay()
    y_third(0)
    y_second(1)
    y_end(0)
    y_third(1)
    for h in range(2):
        z_compute(0, h)
        z_one[0, h].start()
    y_end(1)
    gram_start()
    both(z_one, 0)
    z_compute(1, 0)
    z_compute(1, 1)
    gram_second()
    z_second(0)
    starts(z_two, 0)
    gram_third()
    perm_start()
    starts(z_one, 1)
    gram_fourth()
    z_third(0)
    both(z_one, 1)
    gram_end()
    z_fourth(0)
    factor_block(0)
    z_second(1)
    starts(z_two, 1)
    perm_second()
    both(z_four, 0)
    factor_block(1)
    z_third(1)
    factor_block(2)
    z_fourth(1)
    factor_block(3)
    both(z_four, 1)

    ii = lax.broadcasted_iota(jnp.int32, (512, 512), 0)
    jj = lax.broadcasted_iota(jnp.int32, (512, 512), 1)
    inv_hi, inv_lo = split(jnp.where(ii >= jj, work[...], 0.0))

    def times_inverse(block):
        high, low = split(block)
        parts = []
        for top, k in ((0, 256), (256, 512)):
            h, l = high[:, :k], low[:, :k]
            i_hi, i_lo = inv_hi[top:top + 256, :k], inv_lo[top:top + 256, :k]
            parts.append(mm(h, i_hi, NT) + mm(h, i_lo, NT) + mm(l, i_hi, NT))
        return jnp.concatenate(parts, axis=1)

    copies = []

    def put(src, dst):
        copy = pltpu.make_async_copy(src, dst, osem.at[len(copies)])
        copy.start()
        copies.append(copy)

    z_end(0)
    z_end(1)

    squares = jnp.zeros((512, 1), f32)
    for h in range(2):
        for t in range(2):
            c = slice(t * 512, t * 512 + 512)
            z_hi, z_lo = split(zo[:, h, :, c].reshape(512, 512))
            parts = []
            for top, k in ((0, 256), (256, 512)):
                i_hi, i_lo = inv_hi[top:top + 256, :k], inv_lo[top:top + 256, :k]
                parts.append(mm(i_hi, z_hi[:k]) + mm(i_hi, z_lo[:k]) + mm(i_lo, z_hi[:k]))
            right = jnp.concatenate(parts, axis=0)
            high, low = split(right)
            cols = slice(h * 1024 + t * 512, h * 1024 + t * 512 + 512)
            rt_hi[:, cols] = high
            rt_lo[:, cols] = low
            put(rt_hi.at[:, cols], rt_hi_out.at[:, cols])
            put(rt_lo.at[:, cols], rt_lo_out.at[:, cols])
            squares = squares + jnp.sum(right * right, axis=1, keepdims=True)
    flat = jnp.sum(jnp.where(ii == jj, squares, 0.0), axis=0, keepdims=True)
    csq[...] = jnp.broadcast_to(flat, (8, 512))
    for d in range(1, 8):
        to = (me_col + d) % 8
        send(csq, cfrom.at[me_col], cs.at[d], cr.at[me_col], (me_row, to))

    ortho[...] = (0.05 * times_inverse(power[...])).astype(bf16)
    put(ortho, ortho_out)
    for d in range(1, 8):
        src = (me_col + d) % 8
        arrive(pperm.at[:, ds(src * 16, 16)], p2s.at[d], p2r.at[src])
    served = times_inverse(pperm[...].reshape(768, 512))

    total = csq[...]
    for d in range(1, 8):
        src = (me_col + d) % 8
        arrive(cfrom.at[src], cs.at[d], cr.at[src])
        total = total + cfrom[src]
    root = 1.0 / jnp.sqrt(total + 1e-06)
    scale[...] = root
    put(scale, scale_out)
    coefficient = learn_rate * (ROWS / N) ** 0.5
    high, low = split(served * (-coefficient * root[:1]))
    oph[...] = high
    opl[...] = low
    put(oph, oph_out)
    put(opl, opl_out)
    for copy in copies:
        copy.wait()

    for copy in pending:
        copy.wait_send()


def finish(mom, grad, ortho, oph, opl, rt_hi, rt_lo, scale, new_mom, new_fac, served):
    r_hi, r_lo = rt_hi[...], rt_lo[...]
    new_mom[...] = mom[...] + grad[...].astype(f32) - mm(ortho[...], r_hi)
    served[...] = mm(oph[...], r_hi) + mm(oph[...], r_lo) + mm(opl[...], r_hi)
    new_fac[...] = (r_hi.astype(f32) + r_lo.astype(f32)).T * scale[:1]


def body(momentum, gradient, factor, serve_perm):
    anywhere = pl.BlockSpec(memory_space=pl.ANY)
    V = pltpu.VMEM
    D = pltpu.SemaphoreType.DMA
    shape = jax.ShapeDtypeStruct
    rt_hi, rt_lo, ortho, oph, opl, scale = pl.pallas_call(
        fused,
        out_shape=(shape((512, 2048), bf16), shape((512, 2048), bf16), shape((768, 512), bf16),
                   shape((768, 512), bf16), shape((768, 512), bf16), shape((8, 512), f32)),
        in_specs=[pl.BlockSpec(memory_space=pltpu.SMEM), anywhere, anywhere, anywhere],
        out_specs=(anywhere,) * 6,
        scratch_shapes=[
            V((768, 2048), f32), V((768, 2048), bf16), V((2048, 512), f32),
            V((768, 2048), bf16), V((768, 2048), bf16), V((2048, 512), bf16), V((2048, 512), bf16),
            V((768, 512), f32), V((2, 4, 96, 256), f32), V((2, 4, 96, 256), f32),
            V((2, 2, 48, 256), f32), V((2, 2, 96, 256), f32),
            V((768, 512), f32), V((512, 768), bf16), V((512, 768), bf16),
            V((64, 512), f32), V((16, 8, 256), f32), V((512, 512), f32), V((512, 512), f32),
            V((2, 2, 256, 1024), f32), V((2, 2, 2, 32, 1024), f32), V((2, 2, 2, 64, 1024), f32),
            V((2, 2, 64, 1024), f32), V((2, 2, 3, 16, 1024), f32),
            V((2, 2, 256, 1024), f32),
            V((16, 16, 512), f32), V((16, 16, 512), f32), V((6, 16, 512), f32), V((6, 128, 512), f32),
            V((8, 512), f32), V((8, 8, 512), f32), V((512, 2048), bf16), V((512, 2048), bf16),
            V((768, 512), bf16), V((768, 512), bf16), V((768, 512), bf16), V((8, 512), f32),
            D((2, 3, 8)), D((2, 4)), D((2, 4)), D((2, 2, 6)), D((2, 2, 6)), D((2, 4, 2)), D((2, 4, 2)),
            D((16,)), D((16,)), D((16,)), D((16,)), D((6,)), D((6,)), D((4, 2)), D((4, 2)),
            D((4, 2, 2, 6)), D((4, 2, 2, 6)),
            D((16,)), D((16,)), D((8,)), D((8,)), D((8,)), D((8,)), D((12,)),
        ],
        compiler_params=pltpu.CompilerParams(
            collective_id=0, has_side_effects=True, vmem_limit_bytes=60 * 1024 * 1024),
        name="factorize",
    )(serve_perm, momentum, gradient, factor)

    def tall(i):
        return (0, i)

    def whole(i):
        return (0, 0)

    return pl.pallas_call(
        finish,
        grid=(4,),
        out_shape=(shape((768, 2048), f32), shape((2048, 512), f32), shape((768, 2048), f32)),
        in_specs=[pl.BlockSpec((768, 512), tall), pl.BlockSpec((768, 512), tall),
                  pl.BlockSpec((768, 512), whole), pl.BlockSpec((768, 512), whole),
                  pl.BlockSpec((768, 512), whole),
                  pl.BlockSpec((512, 512), tall), pl.BlockSpec((512, 512), tall),
                  pl.BlockSpec((8, 512), whole)],
        out_specs=(pl.BlockSpec((768, 512), tall), pl.BlockSpec((512, 512), lambda i: (i, 0)),
                   pl.BlockSpec((768, 512), tall)),
        compiler_params=pltpu.CompilerParams(vmem_limit_bytes=60 * 1024 * 1024),
        cost_estimate=pl.CostEstimate(flops=8 * 768 * 2048 * 512, bytes_accessed=30 * 2**20, transcendentals=0),
        name="outputs",
    )(momentum, gradient, ortho, oph, opl, rt_hi, rt_lo, scale)


def solution(mesh):
    return jax.shard_map(
        body,
        mesh=mesh,
        in_specs=(P("row", "col"), P("row", "col"), P("col", None), P()),
        out_specs=(P("row", "col"), P("col", None), P("row", "col")),
        check_vma=False,
    )
```

```python
import jax
import jax.numpy as jnp
from jax import lax
from jax.experimental import pallas as pl
from jax.experimental.pallas import tpu as pltpu
from jax.sharding import PartitionSpec as P

N = 16384
ROWS = 12288
RANK = 512
learn_rate = 0.01

f32 = jnp.float32
bf16 = jnp.bfloat16
HIGHEST = lax.Precision.HIGHEST
MESH = pl.DeviceIdType.MESH
NN = (((1,), (0,)), ((), ()))
NT = (((1,), (1,)), ((), ()))


def mm(a, b, dims=NN):
    return lax.dot_general(a, b, dims, preferred_element_type=f32)


def mm_exact(a, b, dims=NN):
    return lax.dot_general(a, b, dims, precision=HIGHEST, preferred_element_type=f32)


def split(a):
    high = a.astype(bf16)
    return high, (a - high.astype(f32)).astype(bf16)


def eliminate(block, midway):
    lane = lax.broadcasted_iota(jnp.int32, (8, 128), 1)
    sub = lax.broadcasted_iota(jnp.int32, (8, 128), 0)
    done = []
    rest = block
    for first in range(0, 128, 8):
        if first == 40:
            midway()
        height = 128 - first
        cols = [jnp.broadcast_to(rest[:, first + j:first + j + 1], (height, 128)) for j in range(8)]
        inside = (lane >= first) & (lane < first + 8)
        tile = jnp.where(inside, 0.0, rest[:8])
        factors, rows = [], []
        for i in range(8):
            scale = lax.rsqrt(jnp.broadcast_to(cols[i][i:i + 1], (8, 128)))
            column = cols[i] * scale[:1]
            factors.append(column)
            for j in range(i + 1, 8):
                cols[j] = cols[j] - column * column[j:j + 1]
            row = jnp.broadcast_to(jnp.where(lane == first + i, 1.0, tile)[i:i + 1], (8, 128)) * scale
            rows.append(row)
            tile = jnp.where(sub > i, tile - column[:8] * row, jnp.where(sub == i, row, tile))
        done.append(tile)
        if height > 8:
            wide = lax.broadcasted_iota(jnp.int32, (height - 8, 128), 1)
            rest = jnp.where((wide >= first) & (wide < first + 8), 0.0, rest[8:])
            for i in range(8):
                rest = rest - factors[i][8:] * rows[i][:1]
    return jnp.concatenate(done, axis=0)


class Ring:
    def __init__(self, a, peer, ssem, rsem, pending):
        self.a, self.peer, self.ssem, self.rsem, self.pending = a, peer, ssem, rsem, pending
        self.up, self.down, self.far = (a + 1) % 4, (a + 3) % 4, (a + 2) % 4

    def send(self, i, src, dst, to):
        copy = pltpu.make_async_remote_copy(src_ref=src, dst_ref=dst, send_sem=self.ssem(i), recv_sem=self.rsem(i),
                                            device_id=self.peer(to), device_id_type=MESH)
        copy.start()
        self.pending.append(copy)

    def arrive(self, i, dst):
        pltpu.make_async_remote_copy(src_ref=dst, dst_ref=dst, send_sem=self.ssem(i), recv_sem=self.rsem(i),
                                     device_id=self.peer(self.up), device_id_type=MESH).wait_recv()


class Reduce(Ring):
    def bind(self, chunk, relay, land):
        self.chunk, self.relay_ref, self.land = chunk, relay, land
        return self

    def start_far(self):
        self.send(0, self.chunk(self.far, 0), self.relay_ref(0), self.up)
        self.send(1, self.chunk(self.far, 1), self.relay_ref(1), self.down)

    def start_near(self):
        self.send(2, self.chunk(self.up, 1), self.land(0, 1), self.up)
        self.send(3, self.chunk(self.down, 0), self.land(1, 0), self.down)

    def start(self):
        self.start_far()
        self.start_near()

    def relay(self):
        for w, to in ((0, self.up), (1, self.down)):
            ref = self.relay_ref(w)
            self.arrive(w, ref)
            ref[...] = ref[...] + self.chunk(to, w)[...]
            self.send(4 + w, ref, self.land(w, w), to)

    def finish(self, h):
        self.arrive(2 + 1 - h, self.land(1 - h, h))
        self.arrive(4 + h, self.land(h, h))
        return self.chunk(self.a, h)[...] + self.land(0, h)[...] + self.land(1, h)[...]


class Gather(Ring):
    def bind(self, chunk):
        self.chunk = chunk
        return self

    def post(self, i, c, h, to):
        self.send(i, self.chunk(c, h), self.chunk(c, h), to)

    def start(self):
        self.post(0, self.a, 0, self.up)
        self.post(1, self.a, 1, self.down)
        self.post(2, self.a, 1, self.up)
        self.post(3, self.a, 0, self.down)

    def relay(self):
        self.arrive(0, self.chunk(self.down, 0))
        self.post(4, self.down, 0, self.up)
        self.arrive(1, self.chunk(self.up, 1))
        self.post(5, self.up, 1, self.down)

    def finish(self, then=lambda d, h: None):
        for i, d, h in ((2, 3, 1), (3, 1, 0), (4, 2, 0), (5, 2, 1)):
            self.arrive(i, self.chunk((self.a + d) % 4, h))
            then(d, h)


class DirectReduce(Ring):
    def bind(self, chunk, land):
        self.chunk, self.land = chunk, land
        return self

    def start(self):
        for i, to in enumerate((self.far, self.up, self.down)):
            self.send(i, self.chunk(to), self.land(i), to)

    def finish(self):
        total = self.chunk(self.a)[...]
        for i in (1, 2, 0):
            self.arrive(i, self.land(i))
            total = total + self.land(i)[...]
        return total


class DirectGather(Ring):
    def bind(self, chunk):
        self.chunk = chunk
        return self

    def start(self):
        for i, to in enumerate((self.far, self.up, self.down)):
            self.send(i, self.chunk(self.a), self.chunk(self.a), to)

    def finish(self):
        for i, src in ((1, self.down), (2, self.up), (0, self.far)):
            self.arrive(i, self.chunk(src))


def fused(perm_ref, mom_hbm, grad_hbm, fac_hbm,
          rt_hi_out, rt_lo_out, ortho_out, oph_out, opl_out, scale_out,
          mom, grad, fac, buf_hi, buf_lo, fac_hi, fac_lo, part, from_core, to_y, rel_y, land_y,
          power, pt_hi, pt_lo, gpart, gfrom, gram, work, zt, rel1, land1, zsum1, land2, zo,
          psend, pfrom, ppiece, pperm, csq, cfrom, rt_hi, rt_lo, ortho, oph, opl, scale,
          lsem, a1s, a1r, ys, yr, ms, mr, g1s, g1r, g2s, g2r, g3s, g3r, g4s, g4r,
          zs, zr, p1s, p1r, p2s, p2r, cs, cr, osem):
    me_row = lax.axis_index("row")
    me_col = lax.axis_index("col")
    x, z = me_row // 4, me_row % 4
    y, core = me_col // 2, me_col % 2
    mate = (me_row, y * 2 + 1 - core)
    pending = []

    def send(src, dst, ssem, rsem, dev):
        copy = pltpu.make_async_remote_copy(src_ref=src, dst_ref=dst, send_sem=ssem, recv_sem=rsem,
                                            device_id=dev, device_id_type=MESH)
        copy.start()
        pending.append(copy)

    def flush():
        for copy in pending:
            copy.wait_send()
        pending.clear()

    def arrive(dst, ssem, rsem):
        pltpu.make_async_remote_copy(src_ref=dst, dst_ref=dst, send_sem=ssem, recv_sem=rsem,
                                     device_id=mate, device_id_type=MESH).wait_recv()

    def ds(start, size):
        return pl.ds(pl.multiple_of(start, size), size)

    other = pl.multiple_of((1 - core) * 384, 384)
    mine = pl.multiple_of(core * 384, 384)

    def load(h, k):
        rows = pl.ds(other if h == 0 else mine, 384)
        cols = ds(k * 256, 256)
        copies = [pltpu.make_async_copy(mom_hbm.at[rows, cols], mom.at[rows, cols], lsem.at[h, 0, k]),
                  pltpu.make_async_copy(grad_hbm.at[rows, cols], grad.at[rows, cols], lsem.at[h, 1, k])]
        if h == 0:
            copies.append(pltpu.make_async_copy(fac_hbm.at[cols], fac.at[cols], lsem.at[h, 2, k]))
        return copies

    for h in range(2):
        for k in range(8):
            for copy in load(h, k):
                copy.start()

    barrier = pltpu.get_barrier_semaphore()
    for d in range(1, 16):
        pl.semaphore_signal(barrier, inc=1, device_id=((me_row + d) % 16, me_col), device_id_type=MESH)
    for d in range(1, 8):
        pl.semaphore_signal(barrier, inc=1, device_id=(me_row, (me_col + d) % 8), device_id_type=MESH)

    def cols_of(n):
        return slice(n * 256, n * 256 + 256)

    def prepare(h, k):
        for copy in load(h, k):
            copy.wait()
        rows = pl.ds(other if h == 0 else mine, 384)
        cols = ds(k * 256, 256)
        high, low = split(mom[rows, cols] + grad[rows, cols].astype(f32))
        buf_hi[rows, cols] = high
        buf_lo[rows, cols] = low
        if h == 0:
            high, low = split(fac[cols, :])
            fac_hi[cols, :] = high
            fac_lo[cols, :] = low

    def power_block(h, n, k):
        rows = pl.ds(other if h == 0 else mine, 384)
        cols = ds(k * 256, 256)
        c = cols_of(n)
        part[rows, c] = part[rows, c] + (mm(buf_hi[rows, cols], fac_hi[cols, c])
                                         + mm(buf_hi[rows, cols], fac_lo[cols, c])
                                         + mm(buf_lo[rows, cols], fac_hi[cols, c]))

    def power_part(h, n):
        part[pl.ds(other if h == 0 else mine, 384), cols_of(n)] = jnp.zeros((384, 256), f32)
        if n == 0:
            prepare(h, 0)

        @pl.loop(0, 7)
        def _(k):
            if n == 0:
                prepare(h, k + 1)
            power_block(h, n, k)

        power_block(h, n, 7)

    order = (2, 1, 3, 0)

    def core_start(n):
        for d in order:
            to = (y + d) % 4
            send(part.at[ds(other + to * 96, 96), cols_of(n)], from_core.at[n, to],
                 a1s.at[n, d], a1r.at[n, d], mate)

    def core_add(n, d):
        to = (y + d) % 4
        arrive(from_core.at[n, to], a1s.at[n, d], a1r.at[n, d])
        to_y[n, to] = part[ds(mine + to * 96, 96), cols_of(n)] + from_core[n, to]

    def y_peer(to):
        return (me_row, to * 2 + core)

    def half(c, h, size):
        return ds(c * size * 2 + h * size, size)

    def spot(base, c, h):
        return pl.ds(pl.multiple_of(base + c * 96 + h * 48, 48), 48)

    y_sum = [Reduce(y, y_peer, lambda i, n=n: ys.at[0, n, i], lambda i, n=n: yr.at[0, n, i], pending).bind(
        lambda c, h, n=n: to_y.at[n, c, pl.ds(h * 48, 48)],
        lambda w, n=n: rel_y.at[n, w],
        lambda w, h, n=n: land_y.at[n, w, pl.ds(h * 48, 48)]) for n in range(2)]
    y_all = [Gather(y, y_peer, lambda i, n=n: ys.at[1, n, i], lambda i, n=n: yr.at[1, n, i], pending).bind(
        lambda c, h, n=n: power.at[spot(mine, c, h), cols_of(n)]) for n in range(2)]

    def y_start(n):
        core_add(n, 2)
        y_sum[n].start_far()
        core_add(n, 1)
        core_add(n, 3)
        y_sum[n].start_near()

    def to_mate(n, d, h):
        piece = power.at[spot(mine, (y + d) % 4, h), cols_of(n)]
        send(piece, piece, ms.at[n, d, h], mr.at[n, d, h], mate)

    def y_second(n):
        core_add(n, 0)
        for h in range(2):
            power[spot(mine, y, h), cols_of(n)] = y_sum[n].finish(h)
        y_all[n].start()
        for h in range(2):
            to_mate(n, 0, h)

    def y_third(n):
        y_all[n].relay()
        to_mate(n, 3, 0)
        to_mate(n, 1, 1)

    def y_end(n):
        y_all[n].finish(lambda d, h: to_mate(n, d, h))
        for d, h in ((0, 0), (0, 1), (3, 0), (1, 1), (3, 1), (1, 0), (2, 0), (2, 1)):
            piece = power.at[spot(other, (y + d) % 4, h), cols_of(n)]
            arrive(piece, ms.at[n, d, h], mr.at[n, d, h])
        for j in range(6):
            high, low = split(power[j * 128:j * 128 + 128, cols_of(n)].T)
            pt_hi[cols_of(n), j * 128:j * 128 + 128] = high
            pt_lo[cols_of(n), j * 128:j * 128 + 128] = low

    axes = ((x, z), (z, x))

    def z_peer(h, level):
        along_x = (h == 0) == (level == 0)
        return lambda to: (to * 4 + z, me_col) if along_x else (x * 4 + to, me_col)

    def z_sems(stage, n, h):
        return (lambda i: zs.at[stage, n, h, i]), (lambda i: zr.at[stage, n, h, i])

    pairs = [(n, h) for n in range(2) for h in range(2)]
    z_one, z_two, z_three, z_four = {}, {}, {}, {}
    for n, h in pairs:
        a, b = axes[h]
        z_one[n, h] = Reduce(a, z_peer(h, 0), *z_sems(0, n, h), pending).bind(
            lambda c, t, n=n, h=h: zt.at[n, h, half(c, t, 32)],
            lambda w, n=n, h=h: rel1.at[n, h, w],
            lambda w, t, n=n, h=h: land1.at[n, h, w, pl.ds(t * 32, 32)])
        z_two[n, h] = DirectReduce(b, z_peer(h, 1), *z_sems(1, n, h), pending).bind(
            lambda c, n=n, h=h: zsum1.at[n, h, ds(c * 16, 16)],
            lambda i, n=n, h=h: land2.at[n, h, i])
        z_three[n, h] = DirectGather(b, z_peer(h, 1), *z_sems(2, n, h), pending).bind(
            lambda c, n=n, h=h, a=a: zo.at[n, h, ds(a * 64 + c * 16, 16)])
        z_four[n, h] = Gather(a, z_peer(h, 0), *z_sems(3, n, h), pending).bind(
            lambda c, t, n=n, h=h: zo.at[n, h, half(c, t, 32)])

    def z_compute(n, h):
        @pl.loop(0, 2)
        def _(t):
            cols = ds(h * 1024 + t * 512, 512)
            zt[n, h, :, ds(t * 512, 512)] = (
                mm(pt_hi[cols_of(n), :], buf_hi[:, cols]) + mm(pt_hi[cols_of(n), :], buf_lo[:, cols])
                + mm(pt_lo[cols_of(n), :], buf_hi[:, cols]))

    def both(table, n):
        for h in range(2):
            table[n, h].relay()

    def starts(table, n):
        for h in range(2):
            table[n, h].start()

    def z_second(n):
        for h in range(2):
            for t in range(2):
                zsum1[n, h, t * 32:t * 32 + 32, :] = z_one[n, h].finish(t)

    def z_third(n):
        for h in range(2):
            a, b = axes[h]
            zo[n, h, ds(a * 64 + b * 16, 16), :] = z_two[n, h].finish()
            z_three[n, h].start()

    def z_fourth(n):
        for h in range(2):
            z_three[n, h].finish()
            z_four[n, h].start()

    def z_end(n):
        for h in range(2):
            z_four[n, h].finish()

    strip = ds(me_col * 64, 64)

    def unit(r, base=0):
        return (ds(base + (r // 2) * 8, 8), ds((r % 2) * 256, 256))

    def gram_start():
        p_hi, p_lo = pt_hi[strip, :], pt_lo[strip, :]
        gpart[...] = (mm(p_hi, pt_hi[...], NT) + mm(p_hi, pt_lo[...], NT)
                      + mm(p_lo, pt_hi[...], NT) + mm(p_lo, pt_lo[...], NT))
        for d in range(1, 16):
            to = (me_row + d) % 16
            send(gpart.at[unit(to)], gfrom.at[me_row], g1s.at[d], g1r.at[me_row], (to, me_col))

    def gram_second():
        total = gpart[unit(me_row)]
        for d in range(1, 16):
            src = (me_row + d) % 16
            arrive(gfrom.at[src], g1s.at[d], g1r.at[src])
            total = total + gfrom[src]
        gram[unit(me_row, me_col * 64)] = total
        for d in range(1, 16):
            to = (me_row + d) % 16
            piece = gram.at[unit(me_row, me_col * 64)]
            send(piece, piece, g2s.at[d], g2r.at[me_row], (to, me_col))

    def strip_half(c, h, k):
        return gram.at[ds((c * 2 + k) * 64 + h * 32, 32)]

    strips = Gather(y, y_peer, lambda i: g3s.at[i], lambda i: g3r.at[i], pending).bind(
        lambda c, h: strip_half(c, h, core))

    def strip_to_mate(d, h):
        piece = strip_half((y + d) % 4, h, core)
        send(piece, piece, g4s.at[d, h], g4r.at[d, h], mate)

    def gram_third():
        for d in range(1, 16):
            src = (me_row + d) % 16
            arrive(gram.at[unit(src, me_col * 64)], g2s.at[d], g2r.at[src])
        strips.start()
        strip_to_mate(0, 0)
        strip_to_mate(0, 1)

    def gram_fourth():
        strips.relay()
        strip_to_mate(3, 0)
        strip_to_mate(1, 1)

    def gram_end():
        strips.finish(strip_to_mate)
        for d, h in ((0, 0), (0, 1), (3, 0), (1, 1), (3, 1), (1, 0), (2, 0), (2, 1)):
            arrive(strip_half((y + d) % 4, h, 1 - core), g4s.at[d, h], g4r.at[d, h])
        work[...] = gram[...]

    def pick(dest):
        local = jnp.int32(0)
        for t in range(6):
            b = perm_ref[dest * 6 + t] - me_row * 6
            local = local + jnp.where((b >= 0) & (b < 6), b, 0)
        share = power[ds(me_col * 16, 16), :]
        for l in range(1, 6):
            share = jnp.where(local == l, power[ds(l * 128 + me_col * 16, 16), :], share)
        return share

    def perm_start():
        for d in range(1, 16):
            to = (me_row + d) % 16
            psend[d] = pick(to)
            send(psend.at[d], pfrom.at[me_row], p1s.at[d], p1r.at[me_row], (to, me_col))
        pfrom[me_row] = pick(me_row)

    def perm_second():
        for d in range(1, 16):
            src = (me_row + d) % 16
            arrive(pfrom.at[src], p1s.at[d], p1r.at[src])
        for t in range(6):
            first = perm_ref[me_row * 6 + t]
            share = pfrom[0]
            for r in range(1, 16):
                share = jnp.where(first >= r * 6, pfrom[r], share)
            ppiece[t] = share
        mine_rows = ds(me_col * 16, 16)
        pperm[:, mine_rows, :] = ppiece[...]
        for d in range(1, 8):
            to = (me_col + d) % 8
            send(ppiece, pperm.at[:, mine_rows], p2s.at[d], p2r.at[me_col], (me_row, to))

    li = lax.broadcasted_iota(jnp.int32, (128, 128), 0)
    lj = lax.broadcasted_iota(jnp.int32, (128, 128), 1)

    def factor_block(k, midway=lambda: None):
        s = slice(128 * k, 128 * k + 128)
        inv = jnp.where(li >= lj, eliminate(work[s, s], midway), 0.0)
        work[s, s] = jnp.where(li == lj, 1.0, 0.0)
        row = mm_exact(inv, work[s, :])
        work[s, :] = row
        if k < 3:
            r = slice(128 * k + 128, 512)
            low = mm_exact(work[r, s], inv, NT)
            work[r, s] = jnp.zeros((512 - 128 * k - 128, 128), f32)
            work[r, :] = work[r, :] - mm_exact(low, row)

    power_part(0, 0)
    pl.semaphore_wait(barrier, 22)
    core_start(0)
    power_part(1, 0)
    power_part(0, 1)
    core_start(1)
    y_start(0)
    power_part(1, 1)
    y_sum[0].relay()
    y_start(1)
    y_second(0)
    y_sum[1].relay()
    y_third(0)
    y_second(1)
    y_end(0)
    y_third(1)
    for h in range(2):
        z_compute(0, h)
        z_one[0, h].start()
    y_end(1)
    gram_start()
    both(z_one, 0)
    z_compute(1, 0)
    z_compute(1, 1)
    gram_second()
    starts(z_one, 1)
    z_second(0)
    starts(z_two, 0)
    perm_start()
    gram_third()
    both(z_one, 1)
    gram_fourth()
    z_second(1)
    starts(z_two, 1)
    gram_end()
    z_third(0)
    perm_second()
    factor_block(0, lambda: z_third(1))
    z_fourth(0)
    factor_block(1, lambda: z_fourth(1))
    both(z_four, 0)
    factor_block(2, lambda: both(z_four, 1))
    flush()
    factor_block(3)

    ii = lax.broadcasted_iota(jnp.int32, (512, 512), 0)
    jj = lax.broadcasted_iota(jnp.int32, (512, 512), 1)
    inv_hi, inv_lo = split(jnp.where(ii >= jj, work[...], 0.0))

    def times_inverse(block):
        high, low = split(block)
        parts = []
        for top, k in ((0, 256), (256, 512)):
            h, l = high[:, :k], low[:, :k]
            i_hi, i_lo = inv_hi[top:top + 256, :k], inv_lo[top:top + 256, :k]
            parts.append(mm(h, i_hi, NT) + mm(h, i_lo, NT) + mm(l, i_hi, NT))
        return jnp.concatenate(parts, axis=1)

    copies = []

    def put(src, dst):
        copy = pltpu.make_async_copy(src, dst, osem.at[len(copies)])
        copy.start()
        copies.append(copy)

    z_end(0)
    z_end(1)

    squares = jnp.zeros((512, 1), f32)
    for h in range(2):
        for t in range(2):
            c = slice(t * 512, t * 512 + 512)
            z_hi, z_lo = split(zo[:, h, :, c].reshape(512, 512))
            parts = []
            for top, k in ((0, 256), (256, 512)):
                i_hi, i_lo = inv_hi[top:top + 256, :k], inv_lo[top:top + 256, :k]
                parts.append(mm(i_hi, z_hi[:k]) + mm(i_hi, z_lo[:k]) + mm(i_lo, z_hi[:k]))
            right = jnp.concatenate(parts, axis=0)
            high, low = split(right)
            cols = slice(h * 1024 + t * 512, h * 1024 + t * 512 + 512)
            rt_hi[:, cols] = high
            rt_lo[:, cols] = low
            put(rt_hi.at[:, cols], rt_hi_out.at[:, cols])
            put(rt_lo.at[:, cols], rt_lo_out.at[:, cols])
            squares = squares + jnp.sum(right * right, axis=1, keepdims=True)
    flat = jnp.sum(jnp.where(ii == jj, squares, 0.0), axis=0, keepdims=True)
    csq[...] = jnp.broadcast_to(flat, (8, 512))
    for d in range(1, 8):
        to = (me_col + d) % 8
        send(csq, cfrom.at[me_col], cs.at[d], cr.at[me_col], (me_row, to))

    ortho[...] = (0.05 * times_inverse(power[...])).astype(bf16)
    put(ortho, ortho_out)
    for d in range(1, 8):
        src = (me_col + d) % 8
        arrive(pperm.at[:, ds(src * 16, 16)], p2s.at[d], p2r.at[src])
    served = times_inverse(pperm[...].reshape(768, 512))

    total = csq[...]
    for d in range(1, 8):
        src = (me_col + d) % 8
        arrive(cfrom.at[src], cs.at[d], cr.at[src])
        total = total + cfrom[src]
    root = 1.0 / jnp.sqrt(total + 1e-06)
    scale[...] = root
    put(scale, scale_out)
    coefficient = learn_rate * (ROWS / N) ** 0.5
    high, low = split(served * (-coefficient * root[:1]))
    oph[...] = high
    opl[...] = low
    put(oph, oph_out)
    put(opl, opl_out)
    for copy in copies:
        copy.wait()

    for copy in pending:
        copy.wait_send()


def finish(mom, grad, ortho, oph, opl, rt_hi, rt_lo, scale, new_mom, new_fac, served):
    r_hi, r_lo = rt_hi[...], rt_lo[...]
    new_mom[...] = mom[...] + grad[...].astype(f32) - mm(ortho[...], r_hi)
    served[...] = mm(oph[...], r_hi) + mm(oph[...], r_lo) + mm(opl[...], r_hi)
    new_fac[...] = (r_hi.astype(f32) + r_lo.astype(f32)).T * scale[:1]


def body(momentum, gradient, factor, serve_perm):
    anywhere = pl.BlockSpec(memory_space=pl.ANY)
    V = pltpu.VMEM
    D = pltpu.SemaphoreType.DMA
    shape = jax.ShapeDtypeStruct
    rt_hi, rt_lo, ortho, oph, opl, scale = pl.pallas_call(
        fused,
        out_shape=(shape((512, 2048), bf16), shape((512, 2048), bf16), shape((768, 512), bf16),
                   shape((768, 512), bf16), shape((768, 512), bf16), shape((8, 512), f32)),
        in_specs=[pl.BlockSpec(memory_space=pltpu.SMEM), anywhere, anywhere, anywhere],
        out_specs=(anywhere,) * 6,
        scratch_shapes=[
            V((768, 2048), f32), V((768, 2048), bf16), V((2048, 512), f32),
            V((768, 2048), bf16), V((768, 2048), bf16), V((2048, 512), bf16), V((2048, 512), bf16),
            V((768, 512), f32), V((2, 4, 96, 256), f32), V((2, 4, 96, 256), f32),
            V((2, 2, 48, 256), f32), V((2, 2, 96, 256), f32),
            V((768, 512), f32), V((512, 768), bf16), V((512, 768), bf16),
            V((64, 512), f32), V((16, 8, 256), f32), V((512, 512), f32), V((512, 512), f32),
            V((2, 2, 256, 1024), f32), V((2, 2, 2, 32, 1024), f32), V((2, 2, 2, 64, 1024), f32),
            V((2, 2, 64, 1024), f32), V((2, 2, 3, 16, 1024), f32),
            V((2, 2, 256, 1024), f32),
            V((16, 16, 512), f32), V((16, 16, 512), f32), V((6, 16, 512), f32), V((6, 128, 512), f32),
            V((8, 512), f32), V((8, 8, 512), f32), V((512, 2048), bf16), V((512, 2048), bf16),
            V((768, 512), bf16), V((768, 512), bf16), V((768, 512), bf16), V((8, 512), f32),
            D((2, 3, 8)), D((2, 4)), D((2, 4)), D((2, 2, 6)), D((2, 2, 6)), D((2, 4, 2)), D((2, 4, 2)),
            D((16,)), D((16,)), D((16,)), D((16,)), D((6,)), D((6,)), D((4, 2)), D((4, 2)),
            D((4, 2, 2, 6)), D((4, 2, 2, 6)),
            D((16,)), D((16,)), D((8,)), D((8,)), D((8,)), D((8,)), D((12,)),
        ],
        compiler_params=pltpu.CompilerParams(
            collective_id=0, has_side_effects=True, vmem_limit_bytes=60 * 1024 * 1024),
        name="factorize",
    )(serve_perm, momentum, gradient, factor)

    def tall(i):
        return (0, i)

    def whole(i):
        return (0, 0)

    return pl.pallas_call(
        finish,
        grid=(2,),
        out_shape=(shape((768, 2048), f32), shape((2048, 512), f32), shape((768, 2048), f32)),
        in_specs=[pl.BlockSpec((768, 1024), tall), pl.BlockSpec((768, 1024), tall),
                  pl.BlockSpec((768, 512), whole), pl.BlockSpec((768, 512), whole),
                  pl.BlockSpec((768, 512), whole),
                  pl.BlockSpec((512, 1024), tall), pl.BlockSpec((512, 1024), tall),
                  pl.BlockSpec((8, 512), whole)],
        out_specs=(pl.BlockSpec((768, 1024), tall), pl.BlockSpec((1024, 512), lambda i: (i, 0)),
                   pl.BlockSpec((768, 1024), tall)),
        compiler_params=pltpu.CompilerParams(vmem_limit_bytes=60 * 1024 * 1024),
        cost_estimate=pl.CostEstimate(flops=8 * 768 * 2048 * 512, bytes_accessed=30 * 2**20, transcendentals=0),
        name="outputs",
    )(momentum, gradient, ortho, oph, opl, rt_hi, rt_lo, scale)


def solution(mesh):
    return jax.shard_map(
        body,
        mesh=mesh,
        in_specs=(P("row", "col"), P("row", "col"), P("col", None), P()),
        out_specs=(P("row", "col"), P("col", None), P("row", "col")),
        check_vma=False,
    )
```

```python
import jax
import jax.numpy as jnp
from jax import lax
from jax.experimental import pallas as pl
from jax.experimental.pallas import tpu as pltpu
from jax.sharding import PartitionSpec as P

N = 16384
ROWS = 12288
RANK = 512
learn_rate = 0.01

f32 = jnp.float32
bf16 = jnp.bfloat16
HIGHEST = lax.Precision.HIGHEST
MESH = pl.DeviceIdType.MESH
NN = (((1,), (0,)), ((), ()))
NT = (((1,), (1,)), ((), ()))


def mm(a, b, dims=NN):
    return lax.dot_general(a, b, dims, preferred_element_type=f32)


def mm_exact(a, b, dims=NN):
    return lax.dot_general(a, b, dims, precision=HIGHEST, preferred_element_type=f32)


def split(a):
    high = a.astype(bf16)
    return high, (a - high.astype(f32)).astype(bf16)


def eliminate(block, midway):
    lane = lax.broadcasted_iota(jnp.int32, (8, 128), 1)
    sub = lax.broadcasted_iota(jnp.int32, (8, 128), 0)
    done = []
    rest = block
    for first in range(0, 128, 8):
        if first == 40:
            midway()
        height = 128 - first
        cols = [jnp.broadcast_to(rest[:, first + j:first + j + 1], (height, 128)) for j in range(8)]
        inside = (lane >= first) & (lane < first + 8)
        tile = jnp.where(inside, 0.0, rest[:8])
        factors, rows = [], []
        for i in range(8):
            scale = lax.rsqrt(jnp.broadcast_to(cols[i][i:i + 1], (8, 128)))
            column = cols[i] * scale[:1]
            factors.append(column)
            for j in range(i + 1, 8):
                cols[j] = cols[j] - column * column[j:j + 1]
            row = jnp.broadcast_to(jnp.where(lane == first + i, 1.0, tile)[i:i + 1], (8, 128)) * scale
            rows.append(row)
            tile = jnp.where(sub > i, tile - column[:8] * row, jnp.where(sub == i, row, tile))
        done.append(tile)
        if height > 8:
            wide = lax.broadcasted_iota(jnp.int32, (height - 8, 128), 1)
            rest = jnp.where((wide >= first) & (wide < first + 8), 0.0, rest[8:])
            for i in range(8):
                rest = rest - factors[i][8:] * rows[i][:1]
    return jnp.concatenate(done, axis=0)


class Ring:
    def __init__(self, a, peer, ssem, rsem, pending):
        self.a, self.peer, self.ssem, self.rsem, self.pending = a, peer, ssem, rsem, pending
        self.up, self.down, self.far = (a + 1) % 4, (a + 3) % 4, (a + 2) % 4

    def send(self, i, src, dst, to):
        copy = pltpu.make_async_remote_copy(src_ref=src, dst_ref=dst, send_sem=self.ssem(i), recv_sem=self.rsem(i),
                                            device_id=self.peer(to), device_id_type=MESH)
        copy.start()
        self.pending.append(copy)

    def arrive(self, i, dst):
        pltpu.make_async_remote_copy(src_ref=dst, dst_ref=dst, send_sem=self.ssem(i), recv_sem=self.rsem(i),
                                     device_id=self.peer(self.up), device_id_type=MESH).wait_recv()


class Reduce(Ring):
    def bind(self, chunk, relay, land):
        self.chunk, self.relay_ref, self.land = chunk, relay, land
        return self

    def start_far(self):
        self.send(0, self.chunk(self.far, 0), self.relay_ref(0), self.up)
        self.send(1, self.chunk(self.far, 1), self.relay_ref(1), self.down)

    def start_near(self):
        self.send(2, self.chunk(self.up, 1), self.land(0, 1), self.up)
        self.send(3, self.chunk(self.down, 0), self.land(1, 0), self.down)

    def start(self):
        self.start_far()
        self.start_near()

    def relay(self):
        for w, to in ((0, self.up), (1, self.down)):
            ref = self.relay_ref(w)
            self.arrive(w, ref)
            ref[...] = ref[...] + self.chunk(to, w)[...]
            self.send(4 + w, ref, self.land(w, w), to)

    def finish(self, h):
        self.arrive(2 + 1 - h, self.land(1 - h, h))
        self.arrive(4 + h, self.land(h, h))
        return self.chunk(self.a, h)[...] + self.land(0, h)[...] + self.land(1, h)[...]


class Gather(Ring):
    def bind(self, chunk):
        self.chunk = chunk
        return self

    def post(self, i, c, h, to):
        self.send(i, self.chunk(c, h), self.chunk(c, h), to)

    def start(self):
        self.post(0, self.a, 0, self.up)
        self.post(1, self.a, 1, self.down)
        self.post(2, self.a, 1, self.up)
        self.post(3, self.a, 0, self.down)

    def relay(self):
        self.arrive(0, self.chunk(self.down, 0))
        self.post(4, self.down, 0, self.up)
        self.arrive(1, self.chunk(self.up, 1))
        self.post(5, self.up, 1, self.down)

    def finish(self, then=lambda d, h: None):
        for i, d, h in ((2, 3, 1), (3, 1, 0), (4, 2, 0), (5, 2, 1)):
            self.arrive(i, self.chunk((self.a + d) % 4, h))
            then(d, h)


class DirectReduce(Ring):
    def bind(self, chunk, land):
        self.chunk, self.land = chunk, land
        return self

    def start(self):
        for i, to in enumerate((self.far, self.up, self.down)):
            self.send(i, self.chunk(to), self.land(i), to)

    def finish(self):
        total = self.chunk(self.a)[...]
        for i in (1, 2, 0):
            self.arrive(i, self.land(i))
            total = total + self.land(i)[...]
        return total


class DirectGather(Ring):
    def bind(self, chunk):
        self.chunk = chunk
        return self

    def start(self):
        for i, to in enumerate((self.far, self.up, self.down)):
            self.send(i, self.chunk(self.a), self.chunk(self.a), to)

    def finish(self):
        for i, src in ((1, self.down), (2, self.up), (0, self.far)):
            self.arrive(i, self.chunk(src))


def fused(perm_ref, mom_hbm, grad_hbm, fac_hbm,
          rt_hi_out, rt_lo_out, ortho_out, oph_out, opl_out, scale_out,
          mom, grad, fac, buf_hi, buf_lo, fac_hi, fac_lo, part, from_core, to_y, rel_y, land_y,
          power, pt_hi, pt_lo, gpart, gfrom, gram, work, zt, rel1, land1, zsum1, land2, zo,
          psend, pfrom, ppiece, pperm, csq, cfrom, rt_hi, rt_lo, ortho, oph, opl, scale,
          lsem, a1s, a1r, ys, yr, ms, mr, g1s, g1r, g2s, g2r, g3s, g3r, g4s, g4r,
          zs, zr, p1s, p1r, p2s, p2r, cs, cr, osem):
    me_row = lax.axis_index("row")
    me_col = lax.axis_index("col")
    x, z = me_row // 4, me_row % 4
    y, core = me_col // 2, me_col % 2
    mate = (me_row, y * 2 + 1 - core)
    pending = []

    def send(src, dst, ssem, rsem, dev):
        copy = pltpu.make_async_remote_copy(src_ref=src, dst_ref=dst, send_sem=ssem, recv_sem=rsem,
                                            device_id=dev, device_id_type=MESH)
        copy.start()
        pending.append(copy)

    def flush(count):
        for copy in pending[:count]:
            copy.wait_send()
        del pending[:count]

    def arrive(dst, ssem, rsem):
        pltpu.make_async_remote_copy(src_ref=dst, dst_ref=dst, send_sem=ssem, recv_sem=rsem,
                                     device_id=mate, device_id_type=MESH).wait_recv()

    def ds(start, size):
        return pl.ds(pl.multiple_of(start, size), size)

    other = pl.multiple_of((1 - core) * 384, 384)
    mine = pl.multiple_of(core * 384, 384)

    def load(h, k):
        rows = pl.ds(other if h == 0 else mine, 384)
        cols = ds(k * 256, 256)
        copies = [pltpu.make_async_copy(mom_hbm.at[rows, cols], mom.at[rows, cols], lsem.at[h, 0, k]),
                  pltpu.make_async_copy(grad_hbm.at[rows, cols], grad.at[rows, cols], lsem.at[h, 1, k])]
        if h == 0:
            copies.append(pltpu.make_async_copy(fac_hbm.at[cols], fac.at[cols], lsem.at[h, 2, k]))
        return copies

    for h in range(2):
        for k in range(8):
            for copy in load(h, k):
                copy.start()

    barrier = pltpu.get_barrier_semaphore()
    for d in range(1, 16):
        pl.semaphore_signal(barrier, inc=1, device_id=((me_row + d) % 16, me_col), device_id_type=MESH)
    for d in range(1, 8):
        pl.semaphore_signal(barrier, inc=1, device_id=(me_row, (me_col + d) % 8), device_id_type=MESH)

    def cols_of(n):
        return slice(n * 256, n * 256 + 256)

    def prepare(h, k):
        for copy in load(h, k):
            copy.wait()
        rows = pl.ds(other if h == 0 else mine, 384)
        cols = ds(k * 256, 256)
        high, low = split(mom[rows, cols] + grad[rows, cols].astype(f32))
        buf_hi[rows, cols] = high
        buf_lo[rows, cols] = low
        if h == 0:
            high, low = split(fac[cols, :])
            fac_hi[cols, :] = high
            fac_lo[cols, :] = low

    def power_block(h, n, k):
        rows = pl.ds(other if h == 0 else mine, 384)
        cols = ds(k * 256, 256)
        c = cols_of(n)
        part[rows, c] = part[rows, c] + (mm(buf_hi[rows, cols], fac_hi[cols, c])
                                         + mm(buf_hi[rows, cols], fac_lo[cols, c])
                                         + mm(buf_lo[rows, cols], fac_hi[cols, c]))

    def power_part(h, n):
        part[pl.ds(other if h == 0 else mine, 384), cols_of(n)] = jnp.zeros((384, 256), f32)
        if n == 0:
            prepare(h, 0)

        @pl.loop(0, 7)
        def _(k):
            if n == 0:
                prepare(h, k + 1)
            power_block(h, n, k)

        power_block(h, n, 7)

    order = (2, 1, 3, 0)

    def core_start(n):
        for d in order:
            to = (y + d) % 4
            send(part.at[ds(other + to * 96, 96), cols_of(n)], from_core.at[n, to],
                 a1s.at[n, d], a1r.at[n, d], mate)

    def core_add(n, d):
        to = (y + d) % 4
        arrive(from_core.at[n, to], a1s.at[n, d], a1r.at[n, d])
        to_y[n, to] = part[ds(mine + to * 96, 96), cols_of(n)] + from_core[n, to]

    def y_peer(to):
        return (me_row, to * 2 + core)

    def half(c, h, size):
        return ds(c * size * 2 + h * size, size)

    def spot(base, c, h):
        return pl.ds(pl.multiple_of(base + c * 96 + h * 48, 48), 48)

    y_sum = [Reduce(y, y_peer, lambda i, n=n: ys.at[0, n, i], lambda i, n=n: yr.at[0, n, i], pending).bind(
        lambda c, h, n=n: to_y.at[n, c, pl.ds(h * 48, 48)],
        lambda w, n=n: rel_y.at[n, w],
        lambda w, h, n=n: land_y.at[n, w, pl.ds(h * 48, 48)]) for n in range(2)]
    y_all = [Gather(y, y_peer, lambda i, n=n: ys.at[1, n, i], lambda i, n=n: yr.at[1, n, i], pending).bind(
        lambda c, h, n=n: power.at[spot(mine, c, h), cols_of(n)]) for n in range(2)]

    def y_start(n):
        core_add(n, 2)
        y_sum[n].start_far()
        core_add(n, 1)
        core_add(n, 3)
        y_sum[n].start_near()

    def to_mate(n, d, h):
        piece = power.at[spot(mine, (y + d) % 4, h), cols_of(n)]
        send(piece, piece, ms.at[n, d, h], mr.at[n, d, h], mate)

    def y_second(n):
        core_add(n, 0)
        for h in range(2):
            power[spot(mine, y, h), cols_of(n)] = y_sum[n].finish(h)
        y_all[n].start()
        for h in range(2):
            to_mate(n, 0, h)

    def y_third(n):
        y_all[n].relay()
        to_mate(n, 3, 0)
        to_mate(n, 1, 1)

    def y_end(n):
        y_all[n].finish(lambda d, h: to_mate(n, d, h))
        for d, h in ((0, 0), (0, 1), (3, 0), (1, 1), (3, 1), (1, 0), (2, 0), (2, 1)):
            piece = power.at[spot(other, (y + d) % 4, h), cols_of(n)]
            arrive(piece, ms.at[n, d, h], mr.at[n, d, h])
        for j in range(6):
            high, low = split(power[j * 128:j * 128 + 128, cols_of(n)].T)
            pt_hi[cols_of(n), j * 128:j * 128 + 128] = high
            pt_lo[cols_of(n), j * 128:j * 128 + 128] = low

    axes = ((x, z), (z, x))

    def z_peer(h, level):
        along_x = (h == 0) == (level == 0)
        return lambda to: (to * 4 + z, me_col) if along_x else (x * 4 + to, me_col)

    def z_sems(stage, n, h):
        return (lambda i: zs.at[stage, n, h, i]), (lambda i: zr.at[stage, n, h, i])

    pairs = [(n, h) for n in range(2) for h in range(2)]
    z_one, z_two, z_three, z_four = {}, {}, {}, {}
    for n, h in pairs:
        a, b = axes[h]
        z_one[n, h] = Reduce(a, z_peer(h, 0), *z_sems(0, n, h), pending).bind(
            lambda c, t, n=n, h=h: zt.at[n, h, half(c, t, 32)],
            lambda w, n=n, h=h: rel1.at[n, h, w],
            lambda w, t, n=n, h=h: land1.at[n, h, w, pl.ds(t * 32, 32)])
        z_two[n, h] = DirectReduce(b, z_peer(h, 1), *z_sems(1, n, h), pending).bind(
            lambda c, n=n, h=h: zsum1.at[n, h, ds(c * 16, 16)],
            lambda i, n=n, h=h: land2.at[n, h, i])
        z_three[n, h] = DirectGather(b, z_peer(h, 1), *z_sems(2, n, h), pending).bind(
            lambda c, n=n, h=h, a=a: zo.at[n, h, ds(a * 64 + c * 16, 16)])
        z_four[n, h] = Gather(a, z_peer(h, 0), *z_sems(3, n, h), pending).bind(
            lambda c, t, n=n, h=h: zo.at[n, h, half(c, t, 32)])

    def z_compute(n, h):
        @pl.loop(0, 2)
        def _(t):
            cols = ds(h * 1024 + t * 512, 512)
            zt[n, h, :, ds(t * 512, 512)] = (
                mm(pt_hi[cols_of(n), :], buf_hi[:, cols]) + mm(pt_hi[cols_of(n), :], buf_lo[:, cols])
                + mm(pt_lo[cols_of(n), :], buf_hi[:, cols]))

    def both(table, n):
        for h in range(2):
            table[n, h].relay()

    def starts(table, n):
        for h in range(2):
            table[n, h].start()

    def z_second(n):
        for h in range(2):
            for t in range(2):
                zsum1[n, h, t * 32:t * 32 + 32, :] = z_one[n, h].finish(t)

    def z_third(n):
        for h in range(2):
            a, b = axes[h]
            zo[n, h, ds(a * 64 + b * 16, 16), :] = z_two[n, h].finish()
            z_three[n, h].start()

    def z_fourth(n):
        for h in range(2):
            z_three[n, h].finish()
            z_four[n, h].start()

    def z_end(n):
        for h in range(2):
            z_four[n, h].finish()

    strip = ds(me_col * 64, 64)

    def unit(r, base=0):
        return (ds(base + (r // 2) * 8, 8), ds((r % 2) * 256, 256))

    def gram_start():
        p_hi, p_lo = pt_hi[strip, :], pt_lo[strip, :]
        gpart[...] = (mm(p_hi, pt_hi[...], NT) + mm(p_hi, pt_lo[...], NT)
                      + mm(p_lo, pt_hi[...], NT) + mm(p_lo, pt_lo[...], NT))
        for d in range(1, 16):
            to = (me_row + d) % 16
            send(gpart.at[unit(to)], gfrom.at[me_row], g1s.at[d], g1r.at[me_row], (to, me_col))

    def gram_second():
        total = gpart[unit(me_row)]
        for d in range(1, 16):
            src = (me_row + d) % 16
            arrive(gfrom.at[src], g1s.at[d], g1r.at[src])
            total = total + gfrom[src]
        gram[unit(me_row, me_col * 64)] = total
        for d in range(1, 16):
            to = (me_row + d) % 16
            piece = gram.at[unit(me_row, me_col * 64)]
            send(piece, piece, g2s.at[d], g2r.at[me_row], (to, me_col))

    def strip_half(c, h, k):
        return gram.at[ds((c * 2 + k) * 64 + h * 32, 32)]

    strips = Gather(y, y_peer, lambda i: g3s.at[i], lambda i: g3r.at[i], pending).bind(
        lambda c, h: strip_half(c, h, core))

    def strip_to_mate(d, h):
        piece = strip_half((y + d) % 4, h, core)
        send(piece, piece, g4s.at[d, h], g4r.at[d, h], mate)

    def gram_third():
        for d in range(1, 16):
            src = (me_row + d) % 16
            arrive(gram.at[unit(src, me_col * 64)], g2s.at[d], g2r.at[src])
        strips.start()
        strip_to_mate(0, 0)
        strip_to_mate(0, 1)

    def gram_fourth():
        strips.relay()
        strip_to_mate(3, 0)
        strip_to_mate(1, 1)

    def gram_end():
        strips.finish(strip_to_mate)
        for d, h in ((0, 0), (0, 1), (3, 0), (1, 1), (3, 1), (1, 0), (2, 0), (2, 1)):
            arrive(strip_half((y + d) % 4, h, 1 - core), g4s.at[d, h], g4r.at[d, h])
        work[...] = gram[...]

    def pick(dest):
        local = jnp.int32(0)
        for t in range(6):
            b = perm_ref[dest * 6 + t] - me_row * 6
            local = local + jnp.where((b >= 0) & (b < 6), b, 0)
        share = power[ds(me_col * 16, 16), :]
        for l in range(1, 6):
            share = jnp.where(local == l, power[ds(l * 128 + me_col * 16, 16), :], share)
        return share

    def perm_start():
        for d in range(1, 16):
            to = (me_row + d) % 16
            psend[d] = pick(to)
            send(psend.at[d], pfrom.at[me_row], p1s.at[d], p1r.at[me_row], (to, me_col))
        pfrom[me_row] = pick(me_row)

    def perm_second():
        for d in range(1, 16):
            src = (me_row + d) % 16
            arrive(pfrom.at[src], p1s.at[d], p1r.at[src])
        for t in range(6):
            first = perm_ref[me_row * 6 + t]
            share = pfrom[0]
            for r in range(1, 16):
                share = jnp.where(first >= r * 6, pfrom[r], share)
            ppiece[t] = share
        mine_rows = ds(me_col * 16, 16)
        pperm[:, mine_rows, :] = ppiece[...]
        for d in range(1, 8):
            to = (me_col + d) % 8
            send(ppiece, pperm.at[:, mine_rows], p2s.at[d], p2r.at[me_col], (me_row, to))

    li = lax.broadcasted_iota(jnp.int32, (128, 128), 0)
    lj = lax.broadcasted_iota(jnp.int32, (128, 128), 1)

    def factor_block(k, midway=lambda: None):
        s = slice(128 * k, 128 * k + 128)
        inv = jnp.where(li >= lj, eliminate(work[s, s], midway), 0.0)
        work[s, s] = jnp.where(li == lj, 1.0, 0.0)
        row = mm_exact(inv, work[s, :])
        work[s, :] = row
        if k < 3:
            r = slice(128 * k + 128, 512)
            low = mm_exact(work[r, s], inv, NT)
            work[r, s] = jnp.zeros((512 - 128 * k - 128, 128), f32)
            work[r, :] = work[r, :] - mm_exact(low, row)

    power_part(0, 0)
    pl.semaphore_wait(barrier, 22)
    core_start(0)
    power_part(1, 0)
    power_part(0, 1)
    core_start(1)
    y_start(0)
    power_part(1, 1)
    y_sum[0].relay()
    y_start(1)
    y_second(0)
    y_sum[1].relay()
    y_third(0)
    y_second(1)
    y_end(0)
    y_third(1)
    for h in range(2):
        z_compute(0, h)
        z_one[0, h].start()
    y_end(1)
    gram_start()
    both(z_one, 0)
    z_compute(1, 0)
    z_one[1, 0].start()
    z_compute(1, 1)
    z_one[1, 1].start()
    gram_second()
    z_second(0)
    starts(z_two, 0)
    perm_start()
    gram_third()
    both(z_one, 1)
    gram_fourth()
    z_second(1)
    starts(z_two, 1)
    gram_end()
    early = len(pending)
    z_third(0)
    perm_second()
    factor_block(0, lambda: z_third(1))
    z_fourth(0)
    factor_block(1, lambda: z_fourth(1))
    both(z_four, 0)
    factor_block(2, lambda: both(z_four, 1))
    flush(early)
    factor_block(3)

    ii = lax.broadcasted_iota(jnp.int32, (512, 512), 0)
    jj = lax.broadcasted_iota(jnp.int32, (512, 512), 1)
    inv_hi, inv_lo = split(jnp.where(ii >= jj, work[...], 0.0))

    def times_inverse(block):
        high, low = split(block)
        parts = []
        for top, k in ((0, 256), (256, 512)):
            h, l = high[:, :k], low[:, :k]
            i_hi, i_lo = inv_hi[top:top + 256, :k], inv_lo[top:top + 256, :k]
            parts.append(mm(h, i_hi, NT) + mm(h, i_lo, NT) + mm(l, i_hi, NT))
        return jnp.concatenate(parts, axis=1)

    copies = []

    def put(src, dst):
        copy = pltpu.make_async_copy(src, dst, osem.at[len(copies)])
        copy.start()
        copies.append(copy)

    z_end(0)
    z_end(1)

    squares = jnp.zeros((512, 1), f32)
    for h in range(2):
        for t in range(2):
            c = slice(t * 512, t * 512 + 512)
            z_hi, z_lo = split(zo[:, h, :, c].reshape(512, 512))
            parts = []
            for top, k in ((0, 256), (256, 512)):
                i_hi, i_lo = inv_hi[top:top + 256, :k], inv_lo[top:top + 256, :k]
                parts.append(mm(i_hi, z_hi[:k]) + mm(i_hi, z_lo[:k]) + mm(i_lo, z_hi[:k]))
            right = jnp.concatenate(parts, axis=0)
            high, low = split(right)
            cols = slice(h * 1024 + t * 512, h * 1024 + t * 512 + 512)
            rt_hi[:, cols] = high
            rt_lo[:, cols] = low
            put(rt_hi.at[:, cols], rt_hi_out.at[:, cols])
            put(rt_lo.at[:, cols], rt_lo_out.at[:, cols])
            squares = squares + jnp.sum(right * right, axis=1, keepdims=True)
    flat = jnp.sum(jnp.where(ii == jj, squares, 0.0), axis=0, keepdims=True)
    csq[...] = jnp.broadcast_to(flat, (8, 512))
    for d in range(1, 8):
        to = (me_col + d) % 8
        send(csq, cfrom.at[me_col], cs.at[d], cr.at[me_col], (me_row, to))

    ortho[...] = (0.05 * times_inverse(power[...])).astype(bf16)
    put(ortho, ortho_out)
    for d in range(1, 8):
        src = (me_col + d) % 8
        arrive(pperm.at[:, ds(src * 16, 16)], p2s.at[d], p2r.at[src])
    served = times_inverse(pperm[...].reshape(768, 512))

    total = csq[...]
    for d in range(1, 8):
        src = (me_col + d) % 8
        arrive(cfrom.at[src], cs.at[d], cr.at[src])
        total = total + cfrom[src]
    root = 1.0 / jnp.sqrt(total + 1e-06)
    scale[...] = root
    put(scale, scale_out)
    coefficient = learn_rate * (ROWS / N) ** 0.5
    high, low = split(served * (-coefficient * root[:1]))
    oph[...] = high
    opl[...] = low
    put(oph, oph_out)
    put(opl, opl_out)
    for copy in copies:
        copy.wait()

    for copy in pending:
        copy.wait_send()


def finish(mom, grad, ortho, oph, opl, rt_hi, rt_lo, scale, new_mom, new_fac, served):
    r_hi, r_lo = rt_hi[...], rt_lo[...]
    new_mom[...] = mom[...] + grad[...].astype(f32) - mm(ortho[...], r_hi)
    served[...] = mm(oph[...], r_hi) + mm(oph[...], r_lo) + mm(opl[...], r_hi)
    new_fac[...] = (r_hi.astype(f32) + r_lo.astype(f32)).T * scale[:1]


def body(momentum, gradient, factor, serve_perm):
    anywhere = pl.BlockSpec(memory_space=pl.ANY)
    V = pltpu.VMEM
    D = pltpu.SemaphoreType.DMA
    shape = jax.ShapeDtypeStruct
    rt_hi, rt_lo, ortho, oph, opl, scale = pl.pallas_call(
        fused,
        out_shape=(shape((512, 2048), bf16), shape((512, 2048), bf16), shape((768, 512), bf16),
                   shape((768, 512), bf16), shape((768, 512), bf16), shape((8, 512), f32)),
        in_specs=[pl.BlockSpec(memory_space=pltpu.SMEM), anywhere, anywhere, anywhere],
        out_specs=(anywhere,) * 6,
        scratch_shapes=[
            V((768, 2048), f32), V((768, 2048), bf16), V((2048, 512), f32),
            V((768, 2048), bf16), V((768, 2048), bf16), V((2048, 512), bf16), V((2048, 512), bf16),
            V((768, 512), f32), V((2, 4, 96, 256), f32), V((2, 4, 96, 256), f32),
            V((2, 2, 48, 256), f32), V((2, 2, 96, 256), f32),
            V((768, 512), f32), V((512, 768), bf16), V((512, 768), bf16),
            V((64, 512), f32), V((16, 8, 256), f32), V((512, 512), f32), V((512, 512), f32),
            V((2, 2, 256, 1024), f32), V((2, 2, 2, 32, 1024), f32), V((2, 2, 2, 64, 1024), f32),
            V((2, 2, 64, 1024), f32), V((2, 2, 3, 16, 1024), f32),
            V((2, 2, 256, 1024), f32),
            V((16, 16, 512), f32), V((16, 16, 512), f32), V((6, 16, 512), f32), V((6, 128, 512), f32),
            V((8, 512), f32), V((8, 8, 512), f32), V((512, 2048), bf16), V((512, 2048), bf16),
            V((768, 512), bf16), V((768, 512), bf16), V((768, 512), bf16), V((8, 512), f32),
            D((2, 3, 8)), D((2, 4)), D((2, 4)), D((2, 2, 6)), D((2, 2, 6)), D((2, 4, 2)), D((2, 4, 2)),
            D((16,)), D((16,)), D((16,)), D((16,)), D((6,)), D((6,)), D((4, 2)), D((4, 2)),
            D((4, 2, 2, 6)), D((4, 2, 2, 6)),
            D((16,)), D((16,)), D((8,)), D((8,)), D((8,)), D((8,)), D((12,)),
        ],
        compiler_params=pltpu.CompilerParams(
            collective_id=0, has_side_effects=True, vmem_limit_bytes=60 * 1024 * 1024),
        name="factorize",
    )(serve_perm, momentum, gradient, factor)

    def tall(i):
        return (0, i)

    def whole(i):
        return (0, 0)

    return pl.pallas_call(
        finish,
        grid=(2,),
        out_shape=(shape((768, 2048), f32), shape((2048, 512), f32), shape((768, 2048), f32)),
        in_specs=[pl.BlockSpec((768, 1024), tall), pl.BlockSpec((768, 1024), tall),
                  pl.BlockSpec((768, 512), whole), pl.BlockSpec((768, 512), whole),
                  pl.BlockSpec((768, 512), whole),
                  pl.BlockSpec((512, 1024), tall), pl.BlockSpec((512, 1024), tall),
                  pl.BlockSpec((8, 512), whole)],
        out_specs=(pl.BlockSpec((768, 1024), tall), pl.BlockSpec((1024, 512), lambda i: (i, 0)),
                   pl.BlockSpec((768, 1024), tall)),
        compiler_params=pltpu.CompilerParams(vmem_limit_bytes=60 * 1024 * 1024),
        cost_estimate=pl.CostEstimate(flops=8 * 768 * 2048 * 512, bytes_accessed=30 * 2**20, transcendentals=0),
        name="outputs",
    )(momentum, gradient, ortho, oph, opl, rt_hi, rt_lo, scale)


def solution(mesh):
    return jax.shard_map(
        body,
        mesh=mesh,
        in_specs=(P("row", "col"), P("row", "col"), P("col", None), P()),
        out_specs=(P("row", "col"), P("col", None), P("row", "col")),
        check_vma=False,
    )
```
